512 devices in a mesh: blk: 64 (over x, z_lo, core), tp: 8 (over z_hi, y).
Axes of the slice: x: 4, y: 4, z: 16 (z_hi: 2, z_lo: 8; z = z_hi * 8 + z_lo), core: 2. Of those that a mesh axis runs over, the one named last changes fastest.
Arguments:
- weights: float32 [64, 1024, 1024], P('blk', None, 'tp'), may hold values from -6 to 6
- copies: bfloat16 [64, 1024, 1024], P('blk', None, 'tp'), may hold values from -60 to 60
- copies_mixed: bfloat16 [64, 1024, 1024], P('blk', None, 'tp'), may hold values from -64 to 64
- tracker: bfloat16 [64, 1024, 1024], P('blk', None, 'tp'), may hold values from -6 to 6
- tracker_copy: bfloat16 [64, 1024, 1024], P('blk', None, 'tp'), may hold values from -6 to 6
- tracker_mixed: bfloat16 [64, 1024, 1024], P('blk', None, 'tp'), may hold values from -6 to 6
- grad_prev: bfloat16 [64, 1024, 1024], P('blk', None, 'tp'), may hold values from -3 to 3
- tokens: bfloat16 [64, 1024, 1024], P('blk', 'tp'), may hold values from -12 to 12
- image_ids: int32 [64, 1024], P('blk'), may hold values from 0 to 5, never falling along the last dimension, each value on 1 to 197 neighbouring positions
- key_weight: bfloat16 [1024, 1024], P(None, 'tp'), may hold values from -0.1875 to 0.1875
- value_weight: bfloat16 [1024, 1024], P(None, 'tp'), may hold values from -0.1875 to 0.1875
- out_grad: bfloat16 [64, 1024, 1024], P('blk', None, 'tp'), may hold values from -48 to 48
- row_picks: int32 [64, 2, 64], replicated, may hold values from 0 to 1023, as said below
Outputs:
- weights_new: float32 [64, 1024, 1024], P('blk', None, 'tp')
- copies_new: bfloat16 [64, 1024, 1024], P('blk', None, 'tp')
- mixed_new: bfloat16 [64, 1024, 1024], P('blk', None, 'tp')
- tracker_new: bfloat16 [64, 1024, 1024], P('blk', None, 'tp')
- tracker_copy_new: bfloat16 [64, 1024, 1024], P('blk', None, 'tp')
- tracker_mixed_new: bfloat16 [64, 1024, 1024], P('blk', None, 'tp')
- grad_new: bfloat16 [64, 1024, 1024], P('blk', None, 'tp')
- consensus: float32 [], replicated
The draws below stay inside these ranges and needn't reach their ends.
Inputs may be any that keep to these rules, and one draw needn't show every extreme that they name: `image_ids`: never falling along a replica's tokens; an image holds 1 to 197 tokens. `row_picks`: each row lists 64 different rows; the same picks serve every head shard of a replica.
All inputs are finite; a program needn't handle non-finite values.
Results may differ from the reference program's by a relative error of at most 0.0095.
The reference program's roundings to bfloat16 on the way (of `query_weight`, `score_grad` and `query_grad`) count: a program that leaves them out, or rounds other values in their place, can miss the bound.
Values may be sent and summed in bfloat16 or wider, within the bound.
No kernel may reach another device: no remote copies, remote signals or barrier semaphores. Data moves between devices by JAX's collectives and lax.ppermute only.
A program may use at most 64 MiB of HBM per device.

```python
import math
import jax
import jax.numpy as jnp
import numpy as np
from jax import lax

D = 1024
HEADS = 16
HD = 64
SEG_MOST = 197
ROWS = 1024
KBLK = 64
IMGS = 6
N_BLK = 64


def key_matrix(key):
    noise_key = jax.random.fold_in(key, 7002)
    base = jnp.clip(jax.random.normal(noise_key, (D, D), jnp.float32), -6.0, 6.0)
    return (base * D ** (-0.5)).astype(jnp.bfloat16)


def draw_key_weight(key, part):
    return key_matrix(key)


def draw_weights(key, part):
    own_key = jax.random.fold_in(key, 7003)
    full_shape = (N_BLK, D, D)
    return jnp.clip(jax.random.normal(own_key, full_shape, jnp.float32), -6.0, 6.0)


def draw_tokens(key, part):
    own_key = jax.random.fold_in(key, 7004)
    normal_key = jax.random.fold_in(own_key, 0)
    full_shape = (N_BLK, ROWS, D)
    values = jax.random.normal(normal_key, full_shape, jnp.float32)
    return jnp.clip(values, -6.0, 6.0).astype(jnp.bfloat16)


def copy_fields(key):
    base_key = jax.random.fold_in(key, 7010)
    keys_all = jax.random.split(base_key, 8)
    full_shape = (N_BLK, D, D)
    replica = jnp.arange(N_BLK, dtype=jnp.float32)
    level = (1.0 + 2.0 * replica / max(N_BLK - 1, 1)) * jnp.exp(jax.random.uniform(keys_all[0], (N_BLK,), jnp.float32) * jnp.log(1.5))
    column = jnp.arange(D, dtype=jnp.float32) / max(D - 1, 1)
    group_count = D // 16
    rise_groups = jnp.repeat(jnp.exp(jax.random.uniform(keys_all[2], (group_count,), jnp.float32) * jnp.log(2.0)), 16)
    fall_groups = jnp.repeat(jnp.exp(jax.random.uniform(keys_all[3], (group_count,), jnp.float32) * jnp.log(2.0)), 16)
    rising = jnp.exp(jnp.log(6.0) * column) * rise_groups
    falling = jnp.exp(jnp.log(6.0) * (1.0 - column)) * fall_groups
    copy_rows = jnp.exp(jax.random.uniform(keys_all[4], (N_BLK, D, 1), jnp.float32) * jnp.log(3.0))
    gap_rows = jnp.exp(jax.random.uniform(keys_all[5], (N_BLK, D, 1), jnp.float32) * jnp.log(3.0))
    copy_noise = jnp.clip(jax.random.normal(keys_all[6], full_shape, jnp.float32), -4.0, 4.0)
    gap_noise = jnp.clip(jax.random.normal(keys_all[7], full_shape, jnp.float32), -4.0, 4.0)
    copies_value = jnp.clip(0.15 * level[:, None, None] * copy_rows * rising[None, None, :] * copy_noise, -60.0, 60.0)
    gap_value = 0.02 * level[:, None, None] * gap_rows * falling[None, None, :] * gap_noise
    mixed_value = jnp.clip(copies_value + gap_value, -64.0, 64.0)
    return (copies_value, mixed_value)


def draw_copies(key, part):
    copies_value, mixed_value = copy_fields(key)
    return copies_value.astype(jnp.bfloat16)


def draw_copies_mixed(key, part):
    copies_value, mixed_value = copy_fields(key)
    return mixed_value.astype(jnp.bfloat16)


def draw_row_picks(key, part):
    own_key = jax.random.fold_in(key, 7006)
    keys_all = jax.random.split(own_key, N_BLK * 2)
    picked = jax.vmap(lambda single: jax.random.permutation(single, D)[:KBLK])(keys_all)
    return picked.reshape(N_BLK, 2, KBLK).astype(jnp.int32)


def shard_levels(rng, extent, pieces, least, largest):
    def one(dim, parts):
        draws = jax.random.uniform(jax.random.fold_in(jax.random.fold_in(rng, 6), dim), (parts,), jnp.float32, least / len(pieces), largest / len(pieces))
        return jnp.repeat(jnp.exp(draws), extent[dim] // parts).reshape((-1,) + (1,) * (len(extent) - dim - 1))

    factor_of = one(*pieces[0])
    for cut in pieces[1:]:
        factor_of = factor_of * one(*cut)
    return factor_of


def length_profile(amount, total, reach, slope):
    portions = [(1 << 20) // math.isqrt(grade ** slope) + 1 for grade in range(2, amount + 1)]
    surplus, counts = total - reach - (amount - 1), [1] * (amount - 1)
    while surplus > 0:
        free = [i for i in range(amount - 1) if counts[i] < reach]
        mass, remaining = sum([portions[i] for i in free]), surplus
        for i in free:
            extra = min(reach - counts[i], max(1, remaining * portions[i] // mass), surplus)
            counts[i] = counts[i] + extra
            surplus = surplus - extra
    return np.array([reach] + counts)


def ragged(key, number_of, total, bound, slope):
    if number_of == 2:
        one = jax.random.randint(key, (), max(1, total - bound), min(bound, total - 1) + 1)
        return jnp.stack([one, total - one])
    lengths = jnp.asarray(length_profile(number_of, total, bound, slope), jnp.int32)
    twos = (number_of - 1) // 2
    giver, taker = lengths[1:1 + 2 * twos:2], lengths[2:2 + 2 * twos:2]
    margin = jnp.minimum(giver - 1, bound - taker)
    passed = jax.random.randint(jax.random.fold_in(key, 1), (twos,), 0, 1 << 20) % (margin + 1)
    lengths = lengths.at[1:1 + 2 * twos:2].set(giver - passed).at[2:2 + 2 * twos:2].set(taker + passed)
    return lengths[jax.random.permutation(jax.random.fold_in(key, 2), number_of)]


def normal_values(key, extent, scale, reach, pieces=(), held_as=jnp.bfloat16):
    gain = shard_levels(key, extent, pieces, -0.22, 0.18) if pieces else 1.0
    result = jax.random.normal(key, extent, jnp.float32) * scale * gain
    return jnp.minimum(jnp.maximum(result, -reach), reach).astype(held_as)


def setup_inputs(seed: int = 0) -> dict:
    key_list = jax.random.split(jax.random.key(seed), 14)
    weights = draw_weights(jax.random.fold_in(key_list[13], 71), 0)
    copies = draw_copies(jax.random.fold_in(key_list[13], 71), 0)
    copies_mixed = draw_copies_mixed(jax.random.fold_in(key_list[13], 71), 0)
    tracker = normal_values(key_list[3], (N_BLK, D, D), 1.0, 6.0, ((0, 64), (2, 8)))
    tracker_copy = normal_values(key_list[4], (N_BLK, D, D), 1.0, 6.0, ((0, 64), (2, 8)))
    tracker_mixed = normal_values(key_list[5], (N_BLK, D, D), 1.0, 6.0, ((0, 64), (2, 8)))
    grad_prev = normal_values(key_list[6], (N_BLK, D, D), 0.5, 3.0, ((0, 64), (2, 8)))
    tokens = draw_tokens(jax.random.fold_in(key_list[13], 71), 0)
    image_ids = jax.vmap(lambda own: jnp.searchsorted(jnp.cumsum(ragged(own, IMGS, ROWS, SEG_MOST, 0)), jnp.arange(ROWS), side="right"))(jax.random.split(key_list[8], N_BLK)).reshape((N_BLK, ROWS)).astype(jnp.int32)
    key_weight = draw_key_weight(jax.random.fold_in(key_list[13], 71), 0)
    value_weight = normal_values(key_list[10], (D, D), D ** -0.5, 0.1875, ((1, 8),))
    out_grad = normal_values(key_list[11], (N_BLK, ROWS, D), 8.0, 48.0, ((0, 64), (2, 8)))
    row_picks = draw_row_picks(jax.random.fold_in(key_list[13], 71), 0)
    return dict(weights=weights, copies=copies, copies_mixed=copies_mixed, tracker=tracker, tracker_copy=tracker_copy, tracker_mixed=tracker_mixed, grad_prev=grad_prev, tokens=tokens, image_ids=image_ids, key_weight=key_weight, value_weight=value_weight, out_grad=out_grad, row_picks=row_picks)


mixing_rate = 0.2
step_rate = 0.5

def contract(left, right, left_dim, right_dim):
    return lax.dot_general(left.astype(jnp.float32), right.astype(jnp.float32), (((left_dim,), (right_dim,)), ((), ())), preferred_element_type=jnp.float32)

def pick_matrix(picks):
    columns = jnp.arange(D, dtype=jnp.int32)
    return (picks[:, None] == columns[None, :]).astype(jnp.float32)

def compress(picks, field):
    matrix = pick_matrix(picks)
    kept = jnp.dot(matrix, field, precision=lax.Precision.HIGHEST)
    return jnp.dot(matrix.T, kept, precision=lax.Precision.HIGHEST)

def gossip_mix(update):
    return (jnp.roll(update, 1, axis=0) + update + jnp.roll(update, -1, axis=0)) / 3.0

def head_grad(query_head, key_head, value_head, out_head, same_image):
    scores = contract(query_head, key_head, 1, 1) * HD ** (-0.5)
    scores = jnp.where(same_image, scores, -1e+30)
    row_max = lax.optimization_barrier(jnp.max(scores, axis=-1, keepdims=True))
    exponent = jnp.exp(scores - row_max)
    attention = exponent / lax.optimization_barrier(jnp.sum(exponent, axis=-1, keepdims=True))
    out_proj = contract(out_head, value_head, 1, 1)
    centred = out_proj - lax.optimization_barrier(jnp.sum(attention * out_proj, axis=-1, keepdims=True))
    score_grad = (attention * centred * HD ** (-0.5)).astype(jnp.bfloat16)
    return jnp.dot(score_grad.astype(jnp.float32), key_head.astype(jnp.float32), preferred_element_type=jnp.float32).astype(jnp.bfloat16)

def replica_grad(weights_row, token_rows, image_row, out_rows, key_weight, value_weight):
    query_weight = (weights_row * D ** (-0.5)).astype(jnp.bfloat16)
    queries = jnp.dot(token_rows.astype(jnp.float32), query_weight.astype(jnp.float32), preferred_element_type=jnp.float32).astype(jnp.bfloat16)
    keyed = jnp.dot(token_rows.astype(jnp.float32), key_weight.astype(jnp.float32), preferred_element_type=jnp.float32).astype(jnp.bfloat16)
    valued = jnp.dot(token_rows.astype(jnp.float32), value_weight.astype(jnp.float32), preferred_element_type=jnp.float32).astype(jnp.bfloat16)
    same_image = image_row[:, None] == image_row[None, :]
    pieces_list = []
    for head_index in range(HEADS):
        low_col = head_index * HD
        pieces_list.append(head_grad(queries[:, low_col:low_col + HD], keyed[:, low_col:low_col + HD], valued[:, low_col:low_col + HD], out_rows[:, low_col:low_col + HD], same_image))
    query_grad = jnp.concatenate(pieces_list, axis=1)
    return (contract(token_rows, query_grad, 0, 0) * D ** (-0.5)).astype(jnp.bfloat16)

def reference(weights, copies, copies_mixed, tracker, tracker_copy, tracker_mixed, grad_prev, tokens, image_ids, key_weight, value_weight, out_grad, row_picks):
    copy_value = copies.astype(jnp.float32)
    weights_new = weights + mixing_rate * (copies_mixed.astype(jnp.float32) - copy_value) - step_rate * tracker.astype(jnp.float32)
    param_update = jax.vmap(compress)(row_picks[:, 0], weights_new - copy_value)
    copies_new = (copy_value + param_update).astype(jnp.bfloat16)
    mixed_new = (copies_mixed.astype(jnp.float32) + gossip_mix(param_update)).astype(jnp.bfloat16)

    def one_replica(packed):
        return replica_grad(packed[0], packed[1], packed[2], packed[3], key_weight, value_weight)
    grad_new = lax.map(one_replica, (weights_new, tokens, image_ids, out_grad))
    tracker_copy_value = tracker_copy.astype(jnp.float32)
    tracker_new = (tracker.astype(jnp.float32) + mixing_rate * (tracker_mixed.astype(jnp.float32) - tracker_copy_value) + grad_new.astype(jnp.float32) - grad_prev.astype(jnp.float32)).astype(jnp.bfloat16)
    tracker_update = jax.vmap(compress)(row_picks[:, 1], tracker_new.astype(jnp.float32) - tracker_copy_value)
    tracker_copy_new = (tracker_copy_value + tracker_update).astype(jnp.bfloat16)
    tracker_mixed_new = (tracker_mixed.astype(jnp.float32) + gossip_mix(tracker_update)).astype(jnp.bfloat16)
    gap_value = mixed_new.astype(jnp.float32) - copies_new.astype(jnp.float32)
    consensus = jnp.sum(gap_value * gap_value) / (N_BLK * D * D)
    return (weights_new, copies_new, mixed_new, tracker_new, tracker_copy_new, tracker_mixed_new, grad_new, consensus)
```

```python
import jax
import jax.numpy as jnp
from jax import lax
from jax.sharding import Mesh
from jax.sharding import PartitionSpec as P

HD = 64
BLK = ("blk_0", "blk_1", "blk_2")
TP = ("tp_0", "tp_1")


mixing_rate = 0.2
step_rate = 0.5


def swaps(value):
    count = lax.axis_size(BLK)
    near = [(r, r ^ 1) for r in range(count)]
    far = [(r, (r + 1) % count if r % 2 else (r - 1) % count) for r in range(count)]
    return lax.ppermute(value, BLK, near), lax.ppermute(value, BLK, far)


def spread_sum(value, axes):
    count = lax.axis_size(axes)
    rows = jnp.broadcast_to(value, (count, value.shape[1]))
    received = lax.all_to_all(rows, axes, 0, 0, tiled=True)
    return jnp.sum(received, axis=0, keepdims=True)


def spread_tokens(value):
    count = lax.axis_size("tp_1")
    blocks = jnp.broadcast_to(value, (count,) + value.shape[1:])
    return lax.all_to_all(blocks, "tp_1", 0, 0, tiled=True).reshape(-1, value.shape[2])


def join_halves(own_half, other_half):
    low = lax.axis_index("tp_0") == 0
    first = jnp.where(low, own_half, other_half)
    second = jnp.where(low, other_half, own_half)
    return jnp.concatenate([first, second], axis=0)


def contract(left, right, left_dim, right_dim):
    return lax.dot_general(
        left, right, (((left_dim,), (right_dim,)), ((), ())), preferred_element_type=jnp.float32
    )


def pick_matrix(picks, total_rows):
    columns = lax.broadcasted_iota(jnp.int32, (picks.shape[0], total_rows), 1)
    return (picks[:, None] == columns).astype(jnp.float32)


def select_rows(picks, field):
    return jnp.dot(pick_matrix(picks, field.shape[0]), field, precision=lax.Precision.HIGHEST)


def place_rows(picks, values, total_rows):
    matrix = pick_matrix(picks, total_rows)
    return lax.dot_general(
        matrix, values, (((0,), (0,)), ((), ())), precision=lax.Precision.HIGHEST
    )


def neighbour_picks(row_picks, stream):
    replica_count = lax.axis_size(BLK)
    rank = lax.axis_index(BLK)
    near = rank + 1 - 2 * (rank % 2)
    far = (rank - 1 + 2 * (rank % 2) + replica_count) % replica_count
    return jnp.concatenate(
        [
            lax.dynamic_index_in_dim(row_picks, place, 0, keepdims=False)[stream]
            for place in (rank, near, far)
        ],
        axis=0,
    )


def mix_stream(received, row_picks, stream, total_rows):
    picks = neighbour_picks(row_picks, stream)
    return place_rows(picks, received, total_rows) / 3.0


def gap_rows(mixed_new, copies_new):
    gap_value = mixed_new.astype(jnp.float32) - copies_new.astype(jnp.float32)
    return jnp.sum(gap_value * gap_value, axis=0, keepdims=True)


def consensus_of(partial_sums, width):
    total_sum = jnp.sum(spread_sum(partial_sums, ("blk_1", "tp_0")))
    return total_sum / float(lax.axis_size(BLK) * width * width)


def head_grad(query_head, key_head, value_head, out_head, same_image):
    scores = contract(query_head, key_head, 1, 1) * HD ** (-0.5)
    scores = jnp.where(same_image, scores, -1e30)
    row_max = jnp.max(scores, axis=-1, keepdims=True)
    exponent = jnp.exp(scores - row_max)
    attention = exponent / jnp.sum(exponent, axis=-1, keepdims=True)
    out_proj = contract(out_head, value_head, 1, 1)
    centred = out_proj - jnp.sum(attention * out_proj, axis=-1, keepdims=True)
    score_grad = (attention * centred * HD ** (-0.5)).astype(jnp.bfloat16)
    return jnp.dot(score_grad, key_head, preferred_element_type=jnp.float32).astype(jnp.bfloat16)


def attention_grad(projected, image_row, out_rows):
    width = out_rows.shape[1]
    queries = projected[:, :width]
    keyed = projected[:, width : 2 * width]
    valued = projected[:, 2 * width :]
    same_image = image_row[:, None] == image_row[None, :]
    pieces_list = []
    for head_index in range(width // HD):
        low_col = head_index * HD
        pieces_list.append(
            head_grad(
                queries[:, low_col : low_col + HD],
                keyed[:, low_col : low_col + HD],
                valued[:, low_col : low_col + HD],
                out_rows[:, low_col : low_col + HD],
                same_image,
            )
        )
    return jnp.concatenate(pieces_list, axis=1)


def local_gradient(weights_new, gathered, image_ids, key_weight, value_weight, out_grad):
    model_width = weights_new.shape[0]
    query_weight = (weights_new * model_width ** (-0.5)).astype(jnp.bfloat16)
    joined = jnp.concatenate([query_weight, key_weight, value_weight], axis=1)
    projected = jnp.dot(gathered, joined, preferred_element_type=jnp.float32).astype(
        jnp.bfloat16
    )[None][0]
    query_grad = attention_grad(projected, image_ids[0], out_grad[0])
    total = contract(gathered, query_grad, 0, 0)
    return (total * model_width ** (-0.5)).astype(jnp.bfloat16)


def per_device(
    weights,
    copies,
    copies_mixed,
    tracker,
    tracker_copy,
    tracker_mixed,
    grad_prev,
    tokens,
    image_ids,
    key_weight,
    value_weight,
    out_grad,
    row_picks,
):
    model_width = weights.shape[1]
    replica_rank = lax.axis_index(BLK)
    other = lax.ppermute(tokens, "tp_0", [(0, 1), (1, 0)])
    own_half = spread_tokens(tokens)
    own_picks = lax.dynamic_index_in_dim(row_picks, replica_rank, 0, keepdims=False)
    copy_value = copies[0].astype(jnp.float32)
    mixed_value = copies_mixed[0].astype(jnp.float32)
    weights_new = (
        weights[0]
        + mixing_rate * (mixed_value - copy_value)
        - step_rate * tracker[0].astype(jnp.float32)
    )
    param_values = select_rows(own_picks[0], weights_new - copy_value)
    copies_new = (copy_value + place_rows(own_picks[0], param_values, model_width)).astype(
        jnp.bfloat16
    )
    param_sent = param_values.astype(jnp.bfloat16)
    own_half, param_sent = lax.optimization_barrier((own_half, param_sent))
    param_received = jnp.concatenate((param_sent,) + swaps(param_sent), axis=0).astype(jnp.float32)
    mixed_new = (mixed_value + mix_stream(param_received, row_picks, 0, model_width)).astype(
        jnp.bfloat16
    )
    partial_sums = spread_sum(gap_rows(mixed_new, copies_new), ("blk_0", "blk_2", "tp_1"))
    other, partial_sums = lax.optimization_barrier((other, partial_sums))
    other_half = spread_tokens(other)
    gathered = join_halves(own_half, other_half)
    grad_new = local_gradient(weights_new, gathered, image_ids, key_weight, value_weight, out_grad)
    tracker_copy_value = tracker_copy[0].astype(jnp.float32)
    tracker_mixed_value = tracker_mixed[0].astype(jnp.float32)
    tracker_new = (
        tracker[0].astype(jnp.float32)
        + mixing_rate * (tracker_mixed_value - tracker_copy_value)
        + grad_new.astype(jnp.float32)
        - grad_prev[0].astype(jnp.float32)
    ).astype(jnp.bfloat16)
    tracker_values = select_rows(own_picks[1], tracker_new.astype(jnp.float32) - tracker_copy_value)
    tracker_copy_new = (
        tracker_copy_value + place_rows(own_picks[1], tracker_values, model_width)
    ).astype(jnp.bfloat16)
    tracker_values, partial_sums = lax.optimization_barrier((tracker_values, partial_sums))
    consensus = consensus_of(partial_sums, model_width)
    tracker_received = jnp.concatenate((tracker_values,) + swaps(tracker_values), axis=0)
    tracker_mixed_new = (
        tracker_mixed_value + mix_stream(tracker_received, row_picks, 1, model_width)
    ).astype(jnp.bfloat16)
    return (
        weights_new[None],
        copies_new[None],
        mixed_new[None],
        tracker_new[None],
        tracker_copy_new[None],
        tracker_mixed_new[None],
        grad_new[None],
        consensus,
    )


def solution(mesh):
    finer = Mesh(mesh.devices.reshape(4, 8, 2, 2, 4), ("blk_0", "blk_1", "blk_2", "tp_0", "tp_1"))
    in_specs = (
        P(BLK, None, TP),
        P(BLK, None, TP),
        P(BLK, None, TP),
        P(BLK, None, TP),
        P(BLK, None, TP),
        P(BLK, None, TP),
        P(BLK, None, TP),
        P(BLK, TP, None),
        P(BLK, None),
        P(None, TP),
        P(None, TP),
        P(BLK, None, TP),
        P(),
    )
    out_specs = (
        P(BLK, None, TP),
        P(BLK, None, TP),
        P(BLK, None, TP),
        P(BLK, None, TP),
        P(BLK, None, TP),
        P(BLK, None, TP),
        P(BLK, None, TP),
        P(),
    )
    return jax.shard_map(
        per_device, mesh=finer, in_specs=in_specs, out_specs=out_specs, check_vma=False
    )
```

```python
import jax
import jax.numpy as jnp
from jax import lax
from jax.experimental import pallas as pl
from jax.experimental.pallas import tpu as pltpu
from jax.sharding import Mesh
from jax.sharding import PartitionSpec as P

HD = 64
IMAGES = 6
WINDOW = 256
BLK = ("blk_0", "blk_1", "blk_2")
TP = ("tp_0", "tp_1")


mixing_rate = 0.2
step_rate = 0.5


def swaps(value):
    count = lax.axis_size(BLK)
    near = [(r, r ^ 1) for r in range(count)]
    far = [(r, (r + 1) % count if r % 2 else (r - 1) % count) for r in range(count)]
    return lax.ppermute(value, BLK, near), lax.ppermute(value, BLK, far)


def spread_sum(value, axes):
    count = lax.axis_size(axes)
    rows = jnp.broadcast_to(value, (count, value.shape[1]))
    received = lax.all_to_all(rows, axes, 0, 0, tiled=True)
    return jnp.sum(received, axis=0, keepdims=True)


def spread_tokens(value):
    count = lax.axis_size("tp_1")
    blocks = jnp.broadcast_to(value, (count,) + value.shape)
    return lax.all_to_all(blocks, "tp_1", 0, 0, tiled=True).reshape(-1, value.shape[1])


def pass_tokens(value):
    count = lax.axis_size("tp_1")
    blocks = [value]
    for shift in range(1, count):
        pairs = [(i, (i + shift) % count) for i in range(count)]
        blocks.append(lax.ppermute(value, "tp_1", pairs))
    return blocks


def pick_matrix(picks, total_rows):
    columns = lax.broadcasted_iota(jnp.int32, (picks.shape[0], total_rows), 1)
    return (picks[:, None] == columns).astype(jnp.float32)


def select_rows(picks, field):
    return jnp.dot(pick_matrix(picks, field.shape[0]), field, precision=lax.Precision.HIGHEST)


def place_rows(picks, values, total_rows):
    matrix = pick_matrix(picks, total_rows)
    return lax.dot_general(
        matrix, values, (((0,), (0,)), ((), ())), precision=lax.Precision.HIGHEST
    )


def neighbour_picks(row_picks):
    count = lax.axis_size(BLK)
    rank = lax.axis_index(BLK)
    near = rank + 1 - 2 * (rank % 2)
    far = (rank - 1 + 2 * (rank % 2) + count) % count
    return [
        lax.dynamic_index_in_dim(row_picks, place, 0, keepdims=False) for place in (rank, near, far)
    ]


def mix_stream(received, picks, total_rows):
    return place_rows(jnp.concatenate(picks), received, total_rows) / 3.0


def gap_rows(mixed_new, copies_new):
    gap_value = mixed_new.astype(jnp.float32) - copies_new.astype(jnp.float32)
    return jnp.sum(gap_value * gap_value, axis=0, keepdims=True)


def consensus_of(partial_sums, width):
    total_sum = jnp.sum(spread_sum(partial_sums, ("blk_1", "tp_0")))
    return total_sum / float(lax.axis_size(BLK) * width * width)


def image_starts(ids):
    marks = lax.broadcasted_iota(jnp.int32, (8, ids.shape[0]), 0)
    return jnp.sum((ids[None, :] < marks).astype(jnp.int32), axis=1)


def gradient_kernel(
    spots,
    starts,
    picks,
    own,
    other_0,
    other_1,
    other_2,
    other_3,
    query_weight,
    key_weight,
    value_weight,
    out_grad,
    tracker,
    tracker_copy,
    tracker_mixed,
    grad_prev,
    grad_new,
    tracker_new,
    tracker_copy_new,
    update,
    kept,
    joined,
    tokens,
    projected,
    total,
    change,
):
    width = query_weight.shape[1]
    rows = tokens.shape[0]
    joined[:, :width] = query_weight[...]
    joined[:, width : 2 * width] = key_weight[...]
    joined[:, 2 * width :] = value_weight[...]

    def project(block, place):
        size = block.shape[0]
        tokens[pl.ds(place, size), :] = block
        result = jnp.dot(block, joined[...], preferred_element_type=jnp.float32)
        projected[pl.ds(place, size), :] = result.astype(jnp.bfloat16)

    for part in range(own.shape[0] // WINDOW):
        place = pl.multiple_of(spots[0] + part * WINDOW, WINDOW)
        project(own[part * WINDOW : (part + 1) * WINDOW, :], place)
    for index, block in enumerate((other_0, other_1, other_2, other_3)):
        project(block[...], pl.multiple_of(spots[1 + index], 128))
    total[...] = jnp.zeros_like(total)

    lane = lax.broadcasted_iota(jnp.int32, (1, width), 1)
    first_head = (lane < HD).astype(jnp.float32).astype(jnp.bfloat16)
    second_head = (lane >= HD).astype(jnp.float32).astype(jnp.bfloat16)
    scale = HD ** (-0.5)

    @pl.loop(0, IMAGES)
    def _(image):
        start = starts[image]
        end = starts[image + 1]
        base = pl.multiple_of(jnp.minimum((start // 16) * 16, rows - WINDOW), 16)
        window = pl.ds(base, WINDOW)
        query = projected[window, :width] * scale
        keyed = projected[window, width : 2 * width]
        valued = projected[window, 2 * width :]
        given = out_grad[window, :]
        queries = jnp.concatenate([query * first_head, query * second_head], axis=0)
        givens = jnp.concatenate([given * first_head, given * second_head], axis=0)
        over_columns = (((1,), (1,)), ((), ()))
        over_rows = (((0,), (0,)), ((), ()))
        scores = lax.dot_general(keyed, queries, over_columns, preferred_element_type=jnp.float32)
        out_proj = lax.dot_general(valued, givens, over_columns, preferred_element_type=jnp.float32)
        row = lax.broadcasted_iota(jnp.int32, scores.shape, 0) + base
        scores = jnp.where((row >= start) & (row < end), scores, -1e30)
        exponent = jnp.exp(scores - jnp.max(scores, axis=0, keepdims=True))
        inverse = 1.0 / jnp.sum(exponent, axis=0, keepdims=True)
        centre = jnp.sum(exponent * out_proj, axis=0, keepdims=True) * inverse
        score_grad = ((exponent * (inverse * scale)) * (out_proj - centre)).astype(jnp.bfloat16)
        both = lax.dot_general(keyed, score_grad, over_rows, preferred_element_type=jnp.float32)
        query_grad = jnp.concatenate([both[:HD, :WINDOW], both[HD:, WINDOW:]], axis=0)
        column = lax.broadcasted_iota(jnp.int32, query_grad.shape, 1) + base
        query_grad = jnp.where((column >= start) & (column < end), query_grad, 0.0)
        total[...] += jnp.dot(
            query_grad.astype(jnp.bfloat16), tokens[window, :], preferred_element_type=jnp.float32
        )

    gradient = (total[...].T * rows ** (-0.5)).astype(jnp.bfloat16)
    grad_new[...] = gradient
    copy_value = tracker_copy[...].astype(jnp.float32)
    fresh = (
        tracker[...].astype(jnp.float32)
        + mixing_rate * (tracker_mixed[...].astype(jnp.float32) - copy_value)
        + gradient.astype(jnp.float32)
        - grad_prev[...].astype(jnp.float32)
    ).astype(jnp.bfloat16)
    tracker_new[...] = fresh
    change[...] = fresh.astype(jnp.float32) - copy_value
    update[...] = jnp.zeros_like(update)
    for index in range(picks.shape[0]):
        place = picks[index]
        row = change[pl.ds(place, 1), :]
        kept[pl.ds(index, 1), :] = row
        update[pl.ds(place, 1), :] = row
    tracker_copy_new[...] = (copy_value + update[...]).astype(jnp.bfloat16)


def gradient_step(spots, starts, picks, *arrays):
    rows, width = arrays[8].shape
    depth = arrays[0].shape[1]
    scalars = [pl.BlockSpec(memory_space=pltpu.SMEM)] * 3
    whole = pl.BlockSpec(memory_space=pltpu.VMEM)
    narrow = jax.ShapeDtypeStruct((rows, width), jnp.bfloat16)
    return pl.pallas_call(
        gradient_kernel,
        out_shape=(
            narrow,
            narrow,
            narrow,
            jax.ShapeDtypeStruct((rows, width), jnp.float32),
            jax.ShapeDtypeStruct((picks.shape[0], width), jnp.float32),
        ),
        in_specs=scalars + [whole] * len(arrays),
        out_specs=(whole,) * 5,
        scratch_shapes=[
            pltpu.VMEM((depth, 3 * width), jnp.bfloat16),
            pltpu.VMEM((rows, depth), jnp.bfloat16),
            pltpu.VMEM((rows, 3 * width), jnp.bfloat16),
            pltpu.VMEM((width, depth), jnp.float32),
            pltpu.VMEM((rows, width), jnp.float32),
        ],
        compiler_params=pltpu.CompilerParams(vmem_limit_bytes=28 * 2**20),
        cost_estimate=pl.CostEstimate(
            flops=2 * 10**9, bytes_accessed=8 * 10**6, transcendentals=8 * 10**5
        ),
    )(spots, starts, picks, *arrays)


def mix_kernel(near_picks, far_picks, near, far, update, mixed, mixed_new, total):
    total[...] = update[...]
    for picks, values in ((near_picks, near), (far_picks, far)):
        for low in range(0, picks.shape[0], 8):
            places = [pl.ds(picks[low + step], 1) for step in range(8)]
            sums = [
                total[place, :] + values[low + step : low + step + 1, :]
                for step, place in enumerate(places)
            ]
            for place, row in zip(places, sums):
                total[place, :] = row
    mixed_new[...] = (mixed[...].astype(jnp.float32) + total[...] / 3.0).astype(jnp.bfloat16)


def mix_step(near_picks, far_picks, *arrays):
    scalars = [pl.BlockSpec(memory_space=pltpu.SMEM)] * 2
    whole = pl.BlockSpec(memory_space=pltpu.VMEM)
    rows, width = arrays[3].shape
    return pl.pallas_call(
        mix_kernel,
        out_shape=jax.ShapeDtypeStruct((rows, width), jnp.bfloat16),
        in_specs=scalars + [whole] * len(arrays),
        out_specs=whole,
        scratch_shapes=[pltpu.VMEM((rows, width), jnp.float32)],
        compiler_params=pltpu.CompilerParams(vmem_limit_bytes=8 * 2**20),
        cost_estimate=pl.CostEstimate(flops=10**6, bytes_accessed=10**6, transcendentals=0),
    )(near_picks, far_picks, *arrays)


def per_device(
    weights,
    copies,
    copies_mixed,
    tracker,
    tracker_copy,
    tracker_mixed,
    grad_prev,
    tokens,
    image_ids,
    key_weight,
    value_weight,
    out_grad,
    row_picks,
):
    model_width = weights.shape[1]
    high = lax.axis_index("tp_0")
    place = lax.axis_index("tp_1")
    height = tokens.shape[1]
    half = height * lax.axis_size("tp_1")
    other = lax.ppermute(tokens[0], "tp_0", [(0, 1), (1, 0)])
    own_half = spread_tokens(tokens[0])
    picks = neighbour_picks(row_picks)
    own_picks = picks[0]
    copy_value = copies[0].astype(jnp.float32)
    mixed_value = copies_mixed[0].astype(jnp.float32)
    weights_new = (
        weights[0]
        + mixing_rate * (mixed_value - copy_value)
        - step_rate * tracker[0].astype(jnp.float32)
    )
    param_values = select_rows(own_picks[0], weights_new - copy_value)
    copies_new = (copy_value + place_rows(own_picks[0], param_values, model_width)).astype(
        jnp.bfloat16
    )
    param_sent = param_values.astype(jnp.bfloat16)
    param_received = jnp.concatenate((param_sent,) + swaps(param_sent), axis=0).astype(jnp.float32)
    mixed_new = (mixed_value + mix_stream(param_received, [own[0] for own in picks], model_width)).astype(
        jnp.bfloat16
    )
    partial_sums = gap_rows(mixed_new, copies_new)
    own_half, other, partial_sums = lax.optimization_barrier((own_half, other, partial_sums))
    blocks = pass_tokens(other)
    partial_sums = spread_sum(partial_sums, ("blk_0", "blk_2", "tp_1"))
    consensus = consensus_of(partial_sums, model_width)
    spots = [high * half] + [
        (1 - high) * half + ((place - shift) % len(blocks)) * height for shift in range(len(blocks))
    ]
    query_weight = (weights_new * model_width ** (-0.5)).astype(jnp.bfloat16)
    grad_new, tracker_new, tracker_copy_new, update, tracker_values = gradient_step(
        jnp.stack(spots).astype(jnp.int32),
        image_starts(image_ids[0]),
        own_picks[1],
        own_half,
        *blocks,
        query_weight,
        key_weight,
        value_weight,
        out_grad[0],
        tracker[0],
        tracker_copy[0],
        tracker_mixed[0],
        grad_prev[0],
    )
    near, far = swaps(tracker_values)
    tracker_mixed_new = mix_step(picks[1][1], picks[2][1], near, far, update, tracker_mixed[0])
    return (
        weights_new[None],
        copies_new[None],
        mixed_new[None],
        tracker_new[None],
        tracker_copy_new[None],
        tracker_mixed_new[None],
        grad_new[None],
        consensus,
    )


def solution(mesh):
    finer = Mesh(mesh.devices.reshape(4, 8, 2, 2, 4), ("blk_0", "blk_1", "blk_2", "tp_0", "tp_1"))
    in_specs = (
        P(BLK, None, TP),
        P(BLK, None, TP),
        P(BLK, None, TP),
        P(BLK, None, TP),
        P(BLK, None, TP),
        P(BLK, None, TP),
        P(BLK, None, TP),
        P(BLK, TP, None),
        P(BLK, None),
        P(None, TP),
        P(None, TP),
        P(BLK, None, TP),
        P(),
    )
    out_specs = (
        P(BLK, None, TP),
        P(BLK, None, TP),
        P(BLK, None, TP),
        P(BLK, None, TP),
        P(BLK, None, TP),
        P(BLK, None, TP),
        P(BLK, None, TP),
        P(),
    )
    return jax.shard_map(
        per_device, mesh=finer, in_specs=in_specs, out_specs=out_specs, check_vma=False
    )
```

```python
import jax
import jax.numpy as jnp
from jax import lax
from jax.experimental import pallas as pl
from jax.experimental.pallas import tpu as pltpu
from jax.sharding import Mesh
from jax.sharding import PartitionSpec as P

HD = 64
IMAGES = 6
WINDOW = 256
BLK = ("blk_0", "blk_1", "blk_2")
TP = ("tp_0", "tp_1")


mixing_rate = 0.2
step_rate = 0.5


def swaps(value):
    count = lax.axis_size(BLK)
    near = [(r, r ^ 1) for r in range(count)]
    far = [(r, (r + 1) % count if r % 2 else (r - 1) % count) for r in range(count)]
    from_far = lax.ppermute(value, BLK, far)
    return lax.ppermute(value, BLK, near), from_far


def spread_rows(value, axes):
    count = lax.axis_size(axes)
    rows = jnp.broadcast_to(value, (count, value.shape[1]))
    return lax.all_to_all(rows, axes, 0, 0, tiled=True)


def spread_sum(value, axes):
    return jnp.sum(spread_rows(value, axes), axis=0, keepdims=True)


def spread_tokens(value):
    count = lax.axis_size("tp_1")
    blocks = jnp.broadcast_to(value, (count,) + value.shape)
    return lax.all_to_all(blocks, "tp_1", 0, 0, tiled=True).reshape(-1, value.shape[1])


def pass_tokens(value):
    count = lax.axis_size("tp_1")
    blocks = [value]
    for shift in range(1, count):
        pairs = [(i, (i + shift) % count) for i in range(count)]
        blocks.append(lax.ppermute(value, "tp_1", pairs))
    return blocks


def pick_matrix(picks, total_rows):
    columns = lax.broadcasted_iota(jnp.int32, (picks.shape[0], total_rows), 1)
    return (picks[:, None] == columns).astype(jnp.float32)


def select_rows(picks, field):
    return jnp.dot(pick_matrix(picks, field.shape[0]), field, precision=lax.Precision.HIGHEST)


def place_rows(picks, values, total_rows):
    matrix = pick_matrix(picks, total_rows)
    return lax.dot_general(
        matrix, values, (((0,), (0,)), ((), ())), precision=lax.Precision.HIGHEST
    )


def neighbour_picks(row_picks):
    count = lax.axis_size(BLK)
    rank = lax.axis_index(BLK)
    near = rank + 1 - 2 * (rank % 2)
    far = (rank - 1 + 2 * (rank % 2) + count) % count
    return [
        lax.dynamic_index_in_dim(row_picks, place, 0, keepdims=False) for place in (rank, near, far)
    ]


def mix_stream(received, picks, total_rows):
    return place_rows(jnp.concatenate(picks), received, total_rows) / 3.0


def gap_rows(mixed_new, copies_new):
    gap_value = mixed_new.astype(jnp.float32) - copies_new.astype(jnp.float32)
    return jnp.sum(gap_value * gap_value, axis=0, keepdims=True)


def consensus_of(partial_sums, width):
    total_sum = jnp.sum(spread_sum(partial_sums, ("blk_0", "blk_2", "tp_1")))
    return total_sum / float(lax.axis_size(BLK) * width * width)


def image_starts(ids):
    marks = lax.broadcasted_iota(jnp.int32, (8, ids.shape[0]), 0)
    return jnp.sum((ids[None, :] < marks).astype(jnp.int32), axis=1)


def gradient_kernel(
    spots,
    starts,
    picks,
    own,
    other_0,
    other_1,
    other_2,
    other_3,
    query_weight,
    key_weight,
    value_weight,
    out_grad_in,
    tracker_in,
    tracker_copy_in,
    tracker_mixed_in,
    grad_prev_in,
    grad_new,
    tracker_new,
    tracker_copy_new,
    update,
    kept,
    joined,
    tokens,
    projected,
    total,
    change,
    out_grad,
    tracker,
    tracker_copy,
    tracker_mixed,
    grad_prev,
    sems,
):
    width = query_weight.shape[1]
    rows = tokens.shape[0]
    copies = []

    def fetch(source, target):
        copy = pltpu.make_async_copy(source, target, sems.at[len(copies)])
        copy.start()
        copies.append(copy)
        return copy

    ready = [
        fetch(source, joined.at[:, index * width : (index + 1) * width])
        for index, source in enumerate((query_weight, key_weight, value_weight))
    ]
    parts = []
    for part in range(own.shape[0] // WINDOW):
        place = pl.multiple_of(spots[0] + part * WINDOW, WINDOW)
        source = own.at[part * WINDOW : (part + 1) * WINDOW, :]
        parts.append((place, WINDOW, fetch(source, tokens.at[pl.ds(place, WINDOW), :])))
    for index, source in enumerate((other_0, other_1, other_2, other_3)):
        size = source.shape[0]
        place = pl.multiple_of(spots[1 + index], 128)
        parts.append((place, size, fetch(source, tokens.at[pl.ds(place, size), :])))
    given_copy = fetch(out_grad_in, out_grad)
    late = [
        fetch(tracker_in, tracker),
        fetch(tracker_copy_in, tracker_copy),
        fetch(tracker_mixed_in, tracker_mixed),
        fetch(grad_prev_in, grad_prev),
    ]
    for copy in ready:
        copy.wait()
    for place, size, copy in parts:
        copy.wait()
        result = jnp.dot(
            tokens[pl.ds(place, size), :], joined[...], preferred_element_type=jnp.float32
        )
        projected[pl.ds(place, size), :] = result.astype(jnp.bfloat16)
    given_copy.wait()
    total[...] = jnp.zeros_like(total)

    lane = lax.broadcasted_iota(jnp.int32, (1, width), 1)
    first_head = (lane < HD).astype(jnp.float32).astype(jnp.bfloat16)
    second_head = (lane >= HD).astype(jnp.float32).astype(jnp.bfloat16)
    scale = HD ** (-0.5)

    @pl.loop(0, IMAGES)
    def _(image):
        start = starts[image]
        end = starts[image + 1]
        base = pl.multiple_of(jnp.minimum((start // 16) * 16, rows - WINDOW), 16)
        window = pl.ds(base, WINDOW)
        query = projected[window, :width] * scale
        keyed = projected[window, width : 2 * width]
        valued = projected[window, 2 * width :]
        given = out_grad[window, :]
        queries = jnp.concatenate([query * first_head, query * second_head], axis=0)
        givens = jnp.concatenate([given * first_head, given * second_head], axis=0)
        over_columns = (((1,), (1,)), ((), ()))
        over_rows = (((0,), (0,)), ((), ()))
        scores = lax.dot_general(keyed, queries, over_columns, preferred_element_type=jnp.float32)
        out_proj = lax.dot_general(valued, givens, over_columns, preferred_element_type=jnp.float32)
        row = lax.broadcasted_iota(jnp.int32, scores.shape, 0) + base
        scores = jnp.where((row >= start) & (row < end), scores, -1e30)
        exponent = jnp.exp(scores - jnp.max(scores, axis=0, keepdims=True))
        inverse = 1.0 / jnp.sum(exponent, axis=0, keepdims=True)
        centre = jnp.sum(exponent * out_proj, axis=0, keepdims=True) * inverse
        score_grad = ((exponent * (inverse * scale)) * (out_proj - centre)).astype(jnp.bfloat16)
        both = lax.dot_general(keyed, score_grad, over_rows, preferred_element_type=jnp.float32)
        query_grad = jnp.concatenate([both[:HD, :WINDOW], both[HD:, WINDOW:]], axis=0)
        column = lax.broadcasted_iota(jnp.int32, query_grad.shape, 1) + base
        query_grad = jnp.where((column >= start) & (column < end), query_grad, 0.0)
        total[...] += jnp.dot(
            query_grad.astype(jnp.bfloat16), tokens[window, :], preferred_element_type=jnp.float32
        )

    gradient = (total[...].T * rows ** (-0.5)).astype(jnp.bfloat16)
    grad_new[...] = gradient
    for copy in late:
        copy.wait()
    copy_value = tracker_copy[...].astype(jnp.float32)
    fresh = (
        tracker[...].astype(jnp.float32)
        + mixing_rate * (tracker_mixed[...].astype(jnp.float32) - copy_value)
        + gradient.astype(jnp.float32)
        - grad_prev[...].astype(jnp.float32)
    ).astype(jnp.bfloat16)
    tracker_new[...] = fresh
    change[...] = fresh.astype(jnp.float32) - copy_value
    update[...] = jnp.zeros_like(update)
    for index in range(picks.shape[0]):
        place = picks[index]
        row = change[pl.ds(place, 1), :]
        kept[pl.ds(index, 1), :] = row
        update[pl.ds(place, 1), :] = row
    tracker_copy_new[...] = (copy_value + update[...]).astype(jnp.bfloat16)


def gradient_step(spots, starts, picks, *arrays):
    rows, width = arrays[8].shape
    depth = arrays[0].shape[1]
    scalars = [pl.BlockSpec(memory_space=pltpu.SMEM)] * 3
    whole = pl.BlockSpec(memory_space=pltpu.VMEM)
    narrow = jax.ShapeDtypeStruct((rows, width), jnp.bfloat16)
    return pl.pallas_call(
        gradient_kernel,
        out_shape=(
            narrow,
            narrow,
            narrow,
            jax.ShapeDtypeStruct((rows, width), jnp.float32),
            jax.ShapeDtypeStruct((picks.shape[0], width), jnp.float32),
        ),
        in_specs=scalars + [pl.BlockSpec(memory_space=pltpu.HBM)] * len(arrays),
        out_specs=(whole,) * 5,
        scratch_shapes=[
            pltpu.VMEM((depth, 3 * width), jnp.bfloat16),
            pltpu.VMEM((rows, depth), jnp.bfloat16),
            pltpu.VMEM((rows, 3 * width), jnp.bfloat16),
            pltpu.VMEM((width, depth), jnp.float32),
            pltpu.VMEM((rows, width), jnp.float32),
        ]
        + [pltpu.VMEM((rows, width), jnp.bfloat16)] * 5
        + [pltpu.SemaphoreType.DMA((14,))],
        compiler_params=pltpu.CompilerParams(vmem_limit_bytes=56 * 2**20),
        cost_estimate=pl.CostEstimate(
            flops=2 * 10**9, bytes_accessed=8 * 10**6, transcendentals=8 * 10**5
        ),
    )(spots, starts, picks, *arrays)


def mix_kernel(near_picks, far_picks, near, far, update, mixed, mixed_new, total):
    total[...] = update[...]
    for picks, values in ((near_picks, near), (far_picks, far)):
        for low in range(0, picks.shape[0], 8):
            places = [pl.ds(picks[low + step], 1) for step in range(8)]
            sums = [
                total[place, :] + values[low + step : low + step + 1, :]
                for step, place in enumerate(places)
            ]
            for place, row in zip(places, sums):
                total[place, :] = row
    mixed_new[...] = (mixed[...].astype(jnp.float32) + total[...] / 3.0).astype(jnp.bfloat16)


def mix_step(near_picks, far_picks, *arrays):
    scalars = [pl.BlockSpec(memory_space=pltpu.SMEM)] * 2
    whole = pl.BlockSpec(memory_space=pltpu.VMEM)
    rows, width = arrays[3].shape
    return pl.pallas_call(
        mix_kernel,
        out_shape=jax.ShapeDtypeStruct((rows, width), jnp.bfloat16),
        in_specs=scalars + [whole] * len(arrays),
        out_specs=whole,
        scratch_shapes=[pltpu.VMEM((rows, width), jnp.float32)],
        compiler_params=pltpu.CompilerParams(vmem_limit_bytes=8 * 2**20),
        cost_estimate=pl.CostEstimate(flops=10**6, bytes_accessed=10**6, transcendentals=0),
    )(near_picks, far_picks, *arrays)


def per_device(
    weights,
    copies,
    copies_mixed,
    tracker,
    tracker_copy,
    tracker_mixed,
    grad_prev,
    tokens,
    image_ids,
    key_weight,
    value_weight,
    out_grad,
    row_picks,
):
    model_width = weights.shape[1]
    high = lax.axis_index("tp_0")
    place = lax.axis_index("tp_1")
    height = tokens.shape[1]
    half = height * lax.axis_size("tp_1")
    other = lax.ppermute(tokens[0], "tp_0", [(0, 1), (1, 0)])
    own_half = spread_tokens(tokens[0])
    picks = neighbour_picks(row_picks)
    own_picks = picks[0]
    copy_value = copies[0].astype(jnp.float32)
    mixed_value = copies_mixed[0].astype(jnp.float32)
    weights_new = (
        weights[0]
        + mixing_rate * (mixed_value - copy_value)
        - step_rate * tracker[0].astype(jnp.float32)
    )
    param_values = select_rows(own_picks[0], weights_new - copy_value)
    copies_new = (copy_value + place_rows(own_picks[0], param_values, model_width)).astype(
        jnp.bfloat16
    )
    param_sent = param_values.astype(jnp.bfloat16)
    param_received = jnp.concatenate((param_sent,) + swaps(param_sent), axis=0).astype(jnp.float32)
    mixed_new = (mixed_value + mix_stream(param_received, [own[0] for own in picks], model_width)).astype(
        jnp.bfloat16
    )
    partial_sums = gap_rows(mixed_new, copies_new)
    own_half, other = lax.optimization_barrier((own_half, other))
    blocks = pass_tokens(other)
    _, partial_sums = lax.optimization_barrier((other, partial_sums))
    partial_sums = spread_rows(partial_sums, ("blk_1", "tp_0"))
    spots = [high * half] + [
        (1 - high) * half + ((place - shift) % len(blocks)) * height for shift in range(len(blocks))
    ]
    query_weight = (weights_new * model_width ** (-0.5)).astype(jnp.bfloat16)
    grad_new, tracker_new, tracker_copy_new, update, tracker_values = gradient_step(
        jnp.stack(spots).astype(jnp.int32),
        image_starts(image_ids[0]),
        own_picks[1],
        own_half,
        *blocks,
        query_weight,
        key_weight,
        value_weight,
        out_grad[0],
        tracker[0],
        tracker_copy[0],
        tracker_mixed[0],
        grad_prev[0],
    )
    tracker_values, partial_sums = lax.optimization_barrier((tracker_values, partial_sums))
    near, far = swaps(tracker_values)
    consensus = consensus_of(jnp.sum(partial_sums, axis=0, keepdims=True), model_width)
    tracker_mixed_new = mix_step(picks[1][1], picks[2][1], near, far, update, tracker_mixed[0])
    return (
        weights_new[None],
        copies_new[None],
        mixed_new[None],
        tracker_new[None],
        tracker_copy_new[None],
        tracker_mixed_new[None],
        grad_new[None],
        consensus,
    )


def solution(mesh):
    finer = Mesh(mesh.devices.reshape(4, 8, 2, 2, 4), ("blk_0", "blk_1", "blk_2", "tp_0", "tp_1"))
    in_specs = (
        P(BLK, None, TP),
        P(BLK, None, TP),
        P(BLK, None, TP),
        P(BLK, None, TP),
        P(BLK, None, TP),
        P(BLK, None, TP),
        P(BLK, None, TP),
        P(BLK, TP, None),
        P(BLK, None),
        P(None, TP),
        P(None, TP),
        P(BLK, None, TP),
        P(),
    )
    out_specs = (
        P(BLK, None, TP),
        P(BLK, None, TP),
        P(BLK, None, TP),
        P(BLK, None, TP),
        P(BLK, None, TP),
        P(BLK, None, TP),
        P(BLK, None, TP),
        P(),
    )
    return jax.shard_map(
        per_device, mesh=finer, in_specs=in_specs, out_specs=out_specs, check_vma=False
    )
```

```python
import jax
import jax.numpy as jnp
from jax import lax
from jax.experimental import pallas as pl
from jax.experimental.pallas import tpu as pltpu
from jax.sharding import Mesh
from jax.sharding import PartitionSpec as P

HD = 64
IMAGES = 6
WINDOW = 256
BLK = ("blk_0", "blk_1", "blk_2")
TP = ("tp_0", "tp_1")


mixing_rate = 0.2
step_rate = 0.5


def swaps(value):
    count = lax.axis_size(BLK)
    near = [(r, r ^ 1) for r in range(count)]
    far = [(r, (r + 1) % count if r % 2 else (r - 1) % count) for r in range(count)]
    from_far = lax.ppermute(value, BLK, far)
    return lax.ppermute(value, BLK, near), from_far


def spread_rows(value, axes):
    count = lax.axis_size(axes)
    rows = jnp.broadcast_to(value, (count, value.shape[1]))
    return lax.all_to_all(rows, axes, 0, 0, tiled=True)


def spread_sum(value, axes):
    return jnp.sum(spread_rows(value, axes), axis=0, keepdims=True)


def spread_tokens(value):
    count = lax.axis_size("tp_1")
    blocks = jnp.broadcast_to(value, (count,) + value.shape)
    return lax.all_to_all(blocks, "tp_1", 0, 0, tiled=True).reshape(-1, value.shape[1])


def pass_tokens(value):
    count = lax.axis_size("tp_1")
    blocks = [value]
    for shift in range(1, count):
        pairs = [(i, (i + shift) % count) for i in range(count)]
        blocks.append(lax.ppermute(value, "tp_1", pairs))
    return blocks


def pick_matrix(picks, total_rows):
    columns = lax.broadcasted_iota(jnp.int32, (picks.shape[0], total_rows), 1)
    return (picks[:, None] == columns).astype(jnp.float32)


def select_rows(picks, field):
    return jnp.dot(pick_matrix(picks, field.shape[0]), field, precision=lax.Precision.HIGHEST)


def place_rows(picks, values, total_rows):
    matrix = pick_matrix(picks, total_rows)
    return lax.dot_general(
        matrix, values, (((0,), (0,)), ((), ())), precision=lax.Precision.HIGHEST
    )


def neighbour_picks(row_picks):
    count = lax.axis_size(BLK)
    rank = lax.axis_index(BLK)
    near = rank + 1 - 2 * (rank % 2)
    far = (rank - 1 + 2 * (rank % 2) + count) % count
    return [
        lax.dynamic_index_in_dim(row_picks, place, 0, keepdims=False) for place in (rank, near, far)
    ]


def mix_stream(received, picks, total_rows):
    return place_rows(jnp.concatenate(picks), received, total_rows) / 3.0


def gap_rows(mixed_new, copies_new):
    gap_value = mixed_new.astype(jnp.float32) - copies_new.astype(jnp.float32)
    return jnp.sum(gap_value * gap_value, axis=0, keepdims=True)


def consensus_of(partial_sums, width):
    total_sum = jnp.sum(spread_sum(partial_sums, ("blk_1", "tp_0")))
    return total_sum / float(lax.axis_size(BLK) * width * width)


def image_starts(ids):
    marks = lax.broadcasted_iota(jnp.int32, (8, ids.shape[0]), 0)
    return jnp.sum((ids[None, :] < marks).astype(jnp.int32), axis=1)


def gradient_kernel(
    spots,
    starts,
    picks,
    own,
    other_0,
    other_1,
    other_2,
    other_3,
    query_weight,
    key_weight,
    value_weight,
    out_grad_in,
    tracker_in,
    tracker_copy_in,
    tracker_mixed_in,
    grad_prev_in,
    grad_new,
    tracker_new,
    tracker_copy_new,
    update,
    kept,
    joined,
    tokens,
    projected,
    total,
    change,
    out_grad,
    tracker,
    tracker_copy,
    tracker_mixed,
    grad_prev,
    sems,
):
    width = query_weight.shape[1]
    rows = tokens.shape[0]
    copies = []

    def fetch(source, target):
        copy = pltpu.make_async_copy(source, target, sems.at[len(copies)])
        copy.start()
        copies.append(copy)
        return copy

    ready = [
        fetch(source, joined.at[:, index * width : (index + 1) * width])
        for index, source in enumerate((query_weight, key_weight, value_weight))
    ]
    parts = []
    for part in range(own.shape[0] // WINDOW):
        place = pl.multiple_of(spots[0] + part * WINDOW, WINDOW)
        source = own.at[part * WINDOW : (part + 1) * WINDOW, :]
        parts.append((place, WINDOW, fetch(source, tokens.at[pl.ds(place, WINDOW), :])))
    for index, source in enumerate((other_0, other_1, other_2, other_3)):
        size = source.shape[0]
        place = pl.multiple_of(spots[1 + index], 128)
        parts.append((place, size, fetch(source, tokens.at[pl.ds(place, size), :])))
    given_copy = fetch(out_grad_in, out_grad)
    late = [
        fetch(tracker_in, tracker),
        fetch(tracker_copy_in, tracker_copy),
        fetch(tracker_mixed_in, tracker_mixed),
        fetch(grad_prev_in, grad_prev),
    ]
    for copy in ready:
        copy.wait()
    for place, size, copy in parts:
        copy.wait()
        result = jnp.dot(
            tokens[pl.ds(place, size), :], joined[...], preferred_element_type=jnp.float32
        )
        projected[pl.ds(place, size), :] = result.astype(jnp.bfloat16)
    given_copy.wait()
    total[...] = jnp.zeros_like(total)

    lane = lax.broadcasted_iota(jnp.int32, (1, width), 1)
    first_head = (lane < HD).astype(jnp.float32).astype(jnp.bfloat16)
    second_head = (lane >= HD).astype(jnp.float32).astype(jnp.bfloat16)
    scale = HD ** (-0.5)

    @pl.loop(0, IMAGES)
    def _(image):
        start = starts[image]
        end = starts[image + 1]
        base = pl.multiple_of(jnp.minimum((start // 16) * 16, rows - WINDOW), 16)
        window = pl.ds(base, WINDOW)
        query = projected[window, :width] * scale
        keyed = projected[window, width : 2 * width]
        valued = projected[window, 2 * width :]
        given = out_grad[window, :]
        queries = jnp.concatenate([query * first_head, query * second_head], axis=0)
        givens = jnp.concatenate([given * first_head, given * second_head], axis=0)
        over_columns = (((1,), (1,)), ((), ()))
        over_rows = (((0,), (0,)), ((), ()))
        scores = lax.dot_general(keyed, queries, over_columns, preferred_element_type=jnp.float32)
        out_proj = lax.dot_general(valued, givens, over_columns, preferred_element_type=jnp.float32)
        row = lax.broadcasted_iota(jnp.int32, scores.shape, 0) + base
        scores = jnp.where((row >= start) & (row < end), scores, -1e30)
        exponent = jnp.exp(scores - jnp.max(scores, axis=0, keepdims=True))
        inverse = 1.0 / jnp.sum(exponent, axis=0, keepdims=True)
        centre = jnp.sum(exponent * out_proj, axis=0, keepdims=True) * inverse
        score_grad = ((exponent * (inverse * scale)) * (out_proj - centre)).astype(jnp.bfloat16)
        both = lax.dot_general(keyed, score_grad, over_rows, preferred_element_type=jnp.float32)
        query_grad = jnp.concatenate([both[:HD, :WINDOW], both[HD:, WINDOW:]], axis=0)
        column = lax.broadcasted_iota(jnp.int32, query_grad.shape, 1) + base
        query_grad = jnp.where((column >= start) & (column < end), query_grad, 0.0)
        total[...] += jnp.dot(
            query_grad.astype(jnp.bfloat16), tokens[window, :], preferred_element_type=jnp.float32
        )

    gradient = (total[...].T * rows ** (-0.5)).astype(jnp.bfloat16)
    grad_new[...] = gradient
    for copy in late:
        copy.wait()
    copy_value = tracker_copy[...].astype(jnp.float32)
    fresh = (
        tracker[...].astype(jnp.float32)
        + mixing_rate * (tracker_mixed[...].astype(jnp.float32) - copy_value)
        + gradient.astype(jnp.float32)
        - grad_prev[...].astype(jnp.float32)
    ).astype(jnp.bfloat16)
    tracker_new[...] = fresh
    change[...] = fresh.astype(jnp.float32) - copy_value
    update[...] = jnp.zeros_like(update)
    for index in range(picks.shape[0]):
        place = picks[index]
        row = change[pl.ds(place, 1), :]
        kept[pl.ds(index, 1), :] = row
        update[pl.ds(place, 1), :] = row
    tracker_copy_new[...] = (copy_value + update[...]).astype(jnp.bfloat16)


def gradient_step(spots, starts, picks, *arrays):
    rows, width = arrays[8].shape
    depth = arrays[0].shape[1]
    scalars = [pl.BlockSpec(memory_space=pltpu.SMEM)] * 3
    whole = pl.BlockSpec(memory_space=pltpu.VMEM)
    narrow = jax.ShapeDtypeStruct((rows, width), jnp.bfloat16)
    return pl.pallas_call(
        gradient_kernel,
        out_shape=(
            narrow,
            narrow,
            narrow,
            jax.ShapeDtypeStruct((rows, width), jnp.float32),
            jax.ShapeDtypeStruct((picks.shape[0], width), jnp.float32),
        ),
        in_specs=scalars + [pl.BlockSpec(memory_space=pltpu.HBM)] * len(arrays),
        out_specs=(whole,) * 5,
        scratch_shapes=[
            pltpu.VMEM((depth, 3 * width), jnp.bfloat16),
            pltpu.VMEM((rows, depth), jnp.bfloat16),
            pltpu.VMEM((rows, 3 * width), jnp.bfloat16),
            pltpu.VMEM((width, depth), jnp.float32),
            pltpu.VMEM((rows, width), jnp.float32),
        ]
        + [pltpu.VMEM((rows, width), jnp.bfloat16)] * 5
        + [pltpu.SemaphoreType.DMA((14,))],
        compiler_params=pltpu.CompilerParams(vmem_limit_bytes=56 * 2**20),
        cost_estimate=pl.CostEstimate(
            flops=2 * 10**9, bytes_accessed=8 * 10**6, transcendentals=8 * 10**5
        ),
    )(spots, starts, picks, *arrays)


def mix_kernel(far_picks, near_picks, far, near, update, mixed, mixed_new, total):
    total[...] = update[...]
    for picks, values in ((near_picks, near), (far_picks, far)):
        for low in range(0, picks.shape[0], 8):
            places = [pl.ds(picks[low + step], 1) for step in range(8)]
            sums = [
                total[place, :] + values[low + step : low + step + 1, :]
                for step, place in enumerate(places)
            ]
            for place, row in zip(places, sums):
                total[place, :] = row
    mixed_new[...] = (mixed[...].astype(jnp.float32) + total[...] / 3.0).astype(jnp.bfloat16)


def mix_step(far_picks, near_picks, *arrays):
    scalars = [pl.BlockSpec(memory_space=pltpu.SMEM)] * 2
    whole = pl.BlockSpec(memory_space=pltpu.VMEM)
    rows, width = arrays[3].shape
    return pl.pallas_call(
        mix_kernel,
        out_shape=jax.ShapeDtypeStruct((rows, width), jnp.bfloat16),
        in_specs=scalars + [whole] * len(arrays),
        out_specs=whole,
        scratch_shapes=[pltpu.VMEM((rows, width), jnp.float32)],
        compiler_params=pltpu.CompilerParams(vmem_limit_bytes=8 * 2**20),
        cost_estimate=pl.CostEstimate(flops=10**6, bytes_accessed=10**6, transcendentals=0),
    )(far_picks, near_picks, *arrays)


def per_device(
    weights,
    copies,
    copies_mixed,
    tracker,
    tracker_copy,
    tracker_mixed,
    grad_prev,
    tokens,
    image_ids,
    key_weight,
    value_weight,
    out_grad,
    row_picks,
):
    model_width = weights.shape[1]
    high = lax.axis_index("tp_0")
    place = lax.axis_index("tp_1")
    height = tokens.shape[1]
    half = height * lax.axis_size("tp_1")
    other = lax.ppermute(tokens[0], "tp_0", [(0, 1), (1, 0)])
    own_half = spread_tokens(tokens[0])
    picks = neighbour_picks(row_picks)
    own_picks = picks[0]
    copy_value = copies[0].astype(jnp.float32)
    mixed_value = copies_mixed[0].astype(jnp.float32)
    weights_new = (
        weights[0]
        + mixing_rate * (mixed_value - copy_value)
        - step_rate * tracker[0].astype(jnp.float32)
    )
    param_values = select_rows(own_picks[0], weights_new - copy_value)
    copies_new = (copy_value + place_rows(own_picks[0], param_values, model_width)).astype(
        jnp.bfloat16
    )
    param_sent = param_values.astype(jnp.bfloat16)
    param_near, param_far = swaps(param_sent)
    param_received = jnp.concatenate((param_sent, param_far, param_near), axis=0).astype(
        jnp.float32
    )
    mixed_new = (mixed_value + mix_stream(param_received, [own_picks[0], picks[2][0], picks[1][0]], model_width)).astype(
        jnp.bfloat16
    )
    partial_sums = gap_rows(mixed_new, copies_new)
    own_half, other = lax.optimization_barrier((own_half, other))
    blocks = pass_tokens(other)
    _, partial_sums = lax.optimization_barrier((other, partial_sums))
    partial_sums = spread_rows(partial_sums, ("blk_0", "blk_2", "tp_1"))
    spots = [high * half] + [
        (1 - high) * half + ((place - shift) % len(blocks)) * height for shift in range(len(blocks))
    ]
    query_weight = (weights_new * model_width ** (-0.5)).astype(jnp.bfloat16)
    grad_new, tracker_new, tracker_copy_new, update, tracker_values = gradient_step(
        jnp.stack(spots).astype(jnp.int32),
        image_starts(image_ids[0]),
        own_picks[1],
        own_half,
        *blocks,
        query_weight,
        key_weight,
        value_weight,
        out_grad[0],
        tracker[0],
        tracker_copy[0],
        tracker_mixed[0],
        grad_prev[0],
    )
    tracker_values, partial_sums = lax.optimization_barrier((tracker_values, partial_sums))
    near, far = swaps(tracker_values)
    consensus = consensus_of(jnp.sum(partial_sums, axis=0, keepdims=True), model_width)
    tracker_mixed_new = mix_step(picks[2][1], picks[1][1], far, near, update, tracker_mixed[0])
    return (
        weights_new[None],
        copies_new[None],
        mixed_new[None],
        tracker_new[None],
        tracker_copy_new[None],
        tracker_mixed_new[None],
        grad_new[None],
        consensus,
    )


def solution(mesh):
    finer = Mesh(mesh.devices.reshape(4, 8, 2, 2, 4), ("blk_0", "blk_1", "blk_2", "tp_0", "tp_1"))
    in_specs = (
        P(BLK, None, TP),
        P(BLK, None, TP),
        P(BLK, None, TP),
        P(BLK, None, TP),
        P(BLK, None, TP),
        P(BLK, None, TP),
        P(BLK, None, TP),
        P(BLK, TP, None),
        P(BLK, None),
        P(None, TP),
        P(None, TP),
        P(BLK, None, TP),
        P(),
    )
    out_specs = (
        P(BLK, None, TP),
        P(BLK, None, TP),
        P(BLK, None, TP),
        P(BLK, None, TP),
        P(BLK, None, TP),
        P(BLK, None, TP),
        P(BLK, None, TP),
        P(),
    )
    return jax.shard_map(
        per_device, mesh=finer, in_specs=in_specs, out_specs=out_specs, check_vma=False
    )
```

```python
import jax
import jax.numpy as jnp
from jax import lax
from jax.experimental import pallas as pl
from jax.experimental.pallas import tpu as pltpu
from jax.sharding import Mesh
from jax.sharding import PartitionSpec as P

HD = 64
IMAGES = 6
WINDOW = 256
BLK = ("blk_0", "blk_1", "blk_2")
TP = ("tp_0", "tp_1")


mixing_rate = 0.2
step_rate = 0.5


def swaps(value):
    count = lax.axis_size(BLK)
    near = [(r, r ^ 1) for r in range(count)]
    far = [(r, (r + 1) % count if r % 2 else (r - 1) % count) for r in range(count)]
    from_far = lax.ppermute(value, BLK, far)
    return lax.ppermute(value, BLK, near), from_far


def spread_rows(value, axes):
    count = lax.axis_size(axes)
    rows = jnp.broadcast_to(value, (count, value.shape[1]))
    return lax.all_to_all(rows, axes, 0, 0, tiled=True)


def spread_sum(value, axes):
    return jnp.sum(spread_rows(value, axes), axis=0, keepdims=True)


def spread_tokens(value):
    count = lax.axis_size("tp_1")
    blocks = jnp.broadcast_to(value, (count,) + value.shape)
    return lax.all_to_all(blocks, "tp_1", 0, 0, tiled=True).reshape(-1, value.shape[1])


def pass_tokens(value):
    count = lax.axis_size("tp_1")
    blocks = [value]
    for shift in range(1, count):
        pairs = [(i, (i + shift) % count) for i in range(count)]
        blocks.append(lax.ppermute(value, "tp_1", pairs))
    return blocks


def pick_matrix(picks, total_rows):
    columns = lax.broadcasted_iota(jnp.int32, (picks.shape[0], total_rows), 1)
    return (picks[:, None] == columns).astype(jnp.float32)


def select_rows(picks, field):
    return jnp.dot(pick_matrix(picks, field.shape[0]), field, precision=lax.Precision.HIGHEST)


def place_rows(picks, values, total_rows):
    matrix = pick_matrix(picks, total_rows)
    return lax.dot_general(
        matrix, values, (((0,), (0,)), ((), ())), precision=lax.Precision.HIGHEST
    )


def neighbour_picks(row_picks):
    count = lax.axis_size(BLK)
    rank = lax.axis_index(BLK)
    near = rank + 1 - 2 * (rank % 2)
    far = (rank - 1 + 2 * (rank % 2) + count) % count
    return [
        lax.dynamic_index_in_dim(row_picks, place, 0, keepdims=False) for place in (rank, near, far)
    ]


def mix_stream(received, picks, total_rows):
    return place_rows(jnp.concatenate(picks), received, total_rows) / 3.0


def gap_rows(mixed_new, copies_new):
    gap_value = mixed_new.astype(jnp.float32) - copies_new.astype(jnp.float32)
    return jnp.sum(gap_value * gap_value, axis=0, keepdims=True)


def consensus_of(partial_sums, width):
    return jnp.sum(partial_sums) / float(lax.axis_size(BLK) * width * width)


def image_starts(ids):
    marks = lax.broadcasted_iota(jnp.int32, (8, ids.shape[0]), 0)
    return jnp.sum((ids[None, :] < marks).astype(jnp.int32), axis=1)


def gradient_kernel(
    spots,
    starts,
    picks,
    own,
    other_0,
    other_1,
    other_2,
    other_3,
    query_weight,
    key_weight,
    value_weight,
    out_grad_in,
    tracker_in,
    tracker_copy_in,
    tracker_mixed_in,
    grad_prev_in,
    grad_new,
    tracker_new,
    tracker_copy_new,
    update,
    kept,
    joined,
    tokens,
    projected,
    total,
    change,
    out_grad,
    tracker,
    tracker_copy,
    tracker_mixed,
    grad_prev,
    sems,
):
    width = query_weight.shape[1]
    rows = tokens.shape[0]
    copies = []

    def fetch(source, target):
        copy = pltpu.make_async_copy(source, target, sems.at[len(copies)])
        copy.start()
        copies.append(copy)
        return copy

    ready = [
        fetch(source, joined.at[:, index * width : (index + 1) * width])
        for index, source in enumerate((query_weight, key_weight, value_weight))
    ]
    parts = []
    for part in range(own.shape[0] // WINDOW):
        place = pl.multiple_of(spots[0] + part * WINDOW, WINDOW)
        source = own.at[part * WINDOW : (part + 1) * WINDOW, :]
        parts.append(fetch(source, tokens.at[pl.ds(place, WINDOW), :]))
    for index, source in enumerate((other_0, other_1, other_2, other_3)):
        size = source.shape[0]
        place = pl.multiple_of(spots[1 + index], 128)
        parts.append(fetch(source, tokens.at[pl.ds(place, size), :]))
    given_copy = fetch(out_grad_in, out_grad)
    late = [
        fetch(tracker_in, tracker),
        fetch(tracker_copy_in, tracker_copy),
        fetch(tracker_mixed_in, tracker_mixed),
        fetch(grad_prev_in, grad_prev),
    ]
    for copy in ready:
        copy.wait()
    half = own.shape[0]
    for place, group in ((spots[0], parts[:-4]), (half - spots[0], parts[-4:])):
        for copy in group:
            copy.wait()
        window = pl.ds(pl.multiple_of(place, half), half)
        result = jnp.dot(tokens[window, :], joined[...], preferred_element_type=jnp.float32)
        projected[window, :] = result.astype(jnp.bfloat16)
    given_copy.wait()
    total[...] = jnp.zeros_like(total)

    lane = lax.broadcasted_iota(jnp.int32, (1, width), 1)
    first_head = (lane < HD).astype(jnp.float32).astype(jnp.bfloat16)
    second_head = (lane >= HD).astype(jnp.float32).astype(jnp.bfloat16)
    scale = HD ** (-0.5)

    @pl.loop(0, IMAGES, unroll=6)
    def _(image):
        start = starts[image]
        end = starts[image + 1]
        base = pl.multiple_of(jnp.minimum((start // 16) * 16, rows - WINDOW), 16)
        window = pl.ds(base, WINDOW)
        query = projected[window, :width] * scale
        keyed = projected[window, width : 2 * width]
        valued = projected[window, 2 * width :]
        given = out_grad[window, :]
        queries = jnp.concatenate([query * first_head, query * second_head], axis=0)
        givens = jnp.concatenate([given * first_head, given * second_head], axis=0)
        over_columns = (((1,), (1,)), ((), ()))
        over_rows = (((0,), (0,)), ((), ()))
        scores = lax.dot_general(keyed, queries, over_columns, preferred_element_type=jnp.float32)
        out_proj = lax.dot_general(valued, givens, over_columns, preferred_element_type=jnp.float32)
        row = lax.broadcasted_iota(jnp.int32, scores.shape, 0) + base
        scores = jnp.where((row >= start) & (row < end), scores, -1e30)
        exponent = jnp.exp(scores - jnp.max(scores, axis=0, keepdims=True))
        inverse = 1.0 / jnp.sum(exponent, axis=0, keepdims=True)
        centre = jnp.sum(exponent * out_proj, axis=0, keepdims=True) * inverse
        score_grad = ((exponent * (inverse * scale)) * (out_proj - centre)).astype(jnp.bfloat16)
        both = lax.dot_general(keyed, score_grad, over_rows, preferred_element_type=jnp.float32)
        query_grad = jnp.concatenate([both[:HD, :WINDOW], both[HD:, WINDOW:]], axis=0)
        column = lax.broadcasted_iota(jnp.int32, query_grad.shape, 1) + base
        query_grad = jnp.where((column >= start) & (column < end), query_grad, 0.0)
        total[...] += jnp.dot(
            query_grad.astype(jnp.bfloat16), tokens[window, :], preferred_element_type=jnp.float32
        )

    gradient = (total[...].T * rows ** (-0.5)).astype(jnp.bfloat16)
    grad_new[...] = gradient
    for copy in late:
        copy.wait()
    copy_value = tracker_copy[...].astype(jnp.float32)
    fresh = (
        tracker[...].astype(jnp.float32)
        + mixing_rate * (tracker_mixed[...].astype(jnp.float32) - copy_value)
        + gradient.astype(jnp.float32)
        - grad_prev[...].astype(jnp.float32)
    ).astype(jnp.bfloat16)
    tracker_new[...] = fresh
    change[...] = fresh.astype(jnp.float32) - copy_value
    update[...] = jnp.zeros_like(update)
    for index in range(picks.shape[0]):
        place = picks[index]
        row = change[pl.ds(place, 1), :]
        kept[pl.ds(index, 1), :] = row
        update[pl.ds(place, 1), :] = row
    tracker_copy_new[...] = (copy_value + update[...]).astype(jnp.bfloat16)


def gradient_step(spots, starts, picks, *arrays):
    rows, width = arrays[8].shape
    depth = arrays[0].shape[1]
    scalars = [pl.BlockSpec(memory_space=pltpu.SMEM)] * 3
    whole = pl.BlockSpec(memory_space=pltpu.VMEM)
    narrow = jax.ShapeDtypeStruct((rows, width), jnp.bfloat16)
    return pl.pallas_call(
        gradient_kernel,
        out_shape=(
            narrow,
            narrow,
            narrow,
            jax.ShapeDtypeStruct((rows, width), jnp.float32),
            jax.ShapeDtypeStruct((picks.shape[0], width), jnp.float32),
        ),
        in_specs=scalars + [pl.BlockSpec(memory_space=pl.ANY)] * len(arrays),
        out_specs=(whole,) * 5,
        scratch_shapes=[
            pltpu.VMEM((depth, 3 * width), jnp.bfloat16),
            pltpu.VMEM((rows, depth), jnp.bfloat16),
            pltpu.VMEM((rows, 3 * width), jnp.bfloat16),
            pltpu.VMEM((width, depth), jnp.float32),
            pltpu.VMEM((rows, width), jnp.float32),
        ]
        + [pltpu.VMEM((rows, width), jnp.bfloat16)] * 5
        + [pltpu.SemaphoreType.DMA((14,))],
        compiler_params=pltpu.CompilerParams(vmem_limit_bytes=52 * 2**20),
        cost_estimate=pl.CostEstimate(
            flops=2 * 10**9, bytes_accessed=8 * 10**6, transcendentals=8 * 10**5
        ),
    )(spots, starts, picks, *arrays)


def mix_kernel(far_picks, near_picks, far, near, update, mixed, mixed_new, total):
    total[...] = update[...]
    for picks, values in ((near_picks, near), (far_picks, far)):
        for low in range(0, picks.shape[0], 8):
            places = [pl.ds(picks[low + step], 1) for step in range(8)]
            sums = [
                total[place, :] + values[low + step : low + step + 1, :]
                for step, place in enumerate(places)
            ]
            for place, row in zip(places, sums):
                total[place, :] = row
    mixed_new[...] = (mixed[...].astype(jnp.float32) + total[...] / 3.0).astype(jnp.bfloat16)


def mix_step(far_picks, near_picks, *arrays):
    scalars = [pl.BlockSpec(memory_space=pltpu.SMEM)] * 2
    whole = pl.BlockSpec(memory_space=pltpu.VMEM)
    rows, width = arrays[3].shape
    return pl.pallas_call(
        mix_kernel,
        out_shape=jax.ShapeDtypeStruct((rows, width), jnp.bfloat16),
        in_specs=scalars + [whole] * len(arrays),
        out_specs=whole,
        scratch_shapes=[pltpu.VMEM((rows, width), jnp.float32)],
        compiler_params=pltpu.CompilerParams(vmem_limit_bytes=8 * 2**20),
        cost_estimate=pl.CostEstimate(flops=10**6, bytes_accessed=10**6, transcendentals=0),
    )(far_picks, near_picks, *arrays)


def per_device(
    weights,
    copies,
    copies_mixed,
    tracker,
    tracker_copy,
    tracker_mixed,
    grad_prev,
    tokens,
    image_ids,
    key_weight,
    value_weight,
    out_grad,
    row_picks,
):
    model_width = weights.shape[1]
    high = lax.axis_index("tp_0")
    place = lax.axis_index("tp_1")
    height = tokens.shape[1]
    half = height * lax.axis_size("tp_1")
    other = lax.ppermute(tokens[0], "tp_0", [(0, 1), (1, 0)])
    own_half = spread_tokens(tokens[0])
    picks = neighbour_picks(row_picks)
    own_picks = picks[0]
    copy_value = copies[0].astype(jnp.float32)
    mixed_value = copies_mixed[0].astype(jnp.float32)
    weights_new = (
        weights[0]
        + mixing_rate * (mixed_value - copy_value)
        - step_rate * tracker[0].astype(jnp.float32)
    )
    param_values = select_rows(own_picks[0], weights_new - copy_value)
    copies_new = (copy_value + place_rows(own_picks[0], param_values, model_width)).astype(
        jnp.bfloat16
    )
    param_sent = param_values.astype(jnp.bfloat16)
    param_near, param_far = swaps(param_sent)
    param_received = jnp.concatenate((param_sent, param_far, param_near), axis=0).astype(
        jnp.float32
    )
    mixed_new = (mixed_value + mix_stream(param_received, [own_picks[0], picks[2][0], picks[1][0]], model_width)).astype(
        jnp.bfloat16
    )
    partial_sums = gap_rows(mixed_new, copies_new)
    own_half, partial_sums = lax.optimization_barrier((own_half, partial_sums))
    partial_sums = spread_sum(partial_sums, ("blk_0", "blk_2", "tp_1"))
    other, partial_sums = lax.optimization_barrier((other, partial_sums))
    blocks = pass_tokens(other)
    partial_sums = spread_rows(partial_sums, ("blk_1", "tp_0"))
    spots = [high * half] + [
        (1 - high) * half + ((place - shift) % len(blocks)) * height for shift in range(len(blocks))
    ]
    query_weight = (weights_new * model_width ** (-0.5)).astype(jnp.bfloat16)
    grad_new, tracker_new, tracker_copy_new, update, tracker_values = gradient_step(
        jnp.stack(spots).astype(jnp.int32),
        image_starts(image_ids[0]),
        own_picks[1],
        own_half,
        *blocks,
        query_weight,
        key_weight,
        value_weight,
        out_grad[0],
        tracker[0],
        tracker_copy[0],
        tracker_mixed[0],
        grad_prev[0],
    )
    tracker_values, partial_sums = lax.optimization_barrier((tracker_values, partial_sums))
    near, far = swaps(tracker_values)
    consensus = consensus_of(partial_sums, model_width)
    tracker_mixed_new = mix_step(picks[2][1], picks[1][1], far, near, update, tracker_mixed[0])
    return (
        weights_new[None],
        copies_new[None],
        mixed_new[None],
        tracker_new[None],
        tracker_copy_new[None],
        tracker_mixed_new[None],
        grad_new[None],
        consensus,
    )


def solution(mesh):
    finer = Mesh(mesh.devices.reshape(4, 8, 2, 2, 4), ("blk_0", "blk_1", "blk_2", "tp_0", "tp_1"))
    in_specs = (
        P(BLK, None, TP),
        P(BLK, None, TP),
        P(BLK, None, TP),
        P(BLK, None, TP),
        P(BLK, None, TP),
        P(BLK, None, TP),
        P(BLK, None, TP),
        P(BLK, TP, None),
        P(BLK, None),
        P(None, TP),
        P(None, TP),
        P(BLK, None, TP),
        P(),
    )
    out_specs = (
        P(BLK, None, TP),
        P(BLK, None, TP),
        P(BLK, None, TP),
        P(BLK, None, TP),
        P(BLK, None, TP),
        P(BLK, None, TP),
        P(BLK, None, TP),
        P(),
    )
    return jax.shard_map(
        per_device, mesh=finer, in_specs=in_specs, out_specs=out_specs, check_vma=False
    )
```

```python
import jax
import jax.numpy as jnp
from jax import lax
from jax.experimental import pallas as pl
from jax.experimental.pallas import tpu as pltpu
from jax.sharding import Mesh
from jax.sharding import PartitionSpec as P

HD = 64
IMAGES = 6
WINDOW = 256
BLK = ("blk_0", "blk_1", "blk_2")
TP = ("tp_0", "tp_1")


mixing_rate = 0.2
step_rate = 0.5


def swaps(value):
    count = lax.axis_size(BLK)
    near = [(r, r ^ 1) for r in range(count)]
    far = [(r, (r + 1) % count if r % 2 else (r - 1) % count) for r in range(count)]
    from_far = lax.ppermute(value, BLK, far)
    return lax.ppermute(value, BLK, near), from_far


def spread_rows(value, axes):
    count = lax.axis_size(axes)
    rows = jnp.broadcast_to(value, (count, value.shape[1]))
    return lax.all_to_all(rows, axes, 0, 0, tiled=True)


def spread_sum(value, axes):
    return jnp.sum(spread_rows(value, axes), axis=0, keepdims=True)


def spread_tokens(value):
    count = lax.axis_size("tp_1")
    blocks = jnp.broadcast_to(value, (count,) + value.shape)
    return lax.all_to_all(blocks, "tp_1", 0, 0, tiled=True).reshape(-1, value.shape[1])


def pass_tokens(value):
    count = lax.axis_size("tp_1")
    blocks = [value]
    for shift in range(1, count):
        pairs = [(i, (i + shift) % count) for i in range(count)]
        blocks.append(lax.ppermute(value, "tp_1", pairs))
    return blocks


def pick_matrix(picks, total_rows):
    columns = lax.broadcasted_iota(jnp.int32, (picks.shape[0], total_rows), 1)
    return (picks[:, None] == columns).astype(jnp.float32)


def select_rows(picks, field):
    return jnp.dot(pick_matrix(picks, field.shape[0]), field, precision=lax.Precision.HIGHEST)


def place_rows(picks, values, total_rows):
    matrix = pick_matrix(picks, total_rows)
    return lax.dot_general(
        matrix, values, (((0,), (0,)), ((), ())), precision=lax.Precision.HIGHEST
    )


def neighbour_picks(row_picks):
    count = lax.axis_size(BLK)
    rank = lax.axis_index(BLK)
    near = rank + 1 - 2 * (rank % 2)
    far = (rank - 1 + 2 * (rank % 2) + count) % count
    return [
        lax.dynamic_index_in_dim(row_picks, place, 0, keepdims=False) for place in (rank, near, far)
    ]


def mix_stream(received, picks, total_rows):
    return place_rows(jnp.concatenate(picks), received, total_rows) / 3.0


def gap_rows(mixed_new, copies_new):
    gap_value = mixed_new.astype(jnp.float32) - copies_new.astype(jnp.float32)
    return jnp.sum(gap_value * gap_value, axis=0, keepdims=True)


def consensus_of(partial_sums, width):
    return jnp.sum(partial_sums) / float(lax.axis_size(BLK) * width * width)


def image_starts(ids):
    marks = lax.broadcasted_iota(jnp.int32, (8, ids.shape[0]), 0)
    return jnp.sum((ids[None, :] < marks).astype(jnp.int32), axis=1)


def gradient_kernel(
    spots,
    starts,
    picks,
    own,
    other_0,
    other_1,
    other_2,
    other_3,
    query_weight,
    key_weight,
    value_weight,
    out_grad_in,
    tracker_in,
    tracker_copy_in,
    tracker_mixed_in,
    grad_prev_in,
    grad_new,
    tracker_new,
    tracker_copy_new,
    update,
    kept,
    joined,
    tokens,
    projected,
    total,
    change,
    out_grad,
    tracker,
    tracker_copy,
    tracker_mixed,
    grad_prev,
    sems,
):
    width = query_weight.shape[1]
    rows = tokens.shape[0]
    copies = []

    def fetch(source, target):
        copy = pltpu.make_async_copy(source, target, sems.at[len(copies)])
        copy.start()
        copies.append(copy)
        return copy

    ready = [
        fetch(source, joined.at[:, index * width : (index + 1) * width])
        for index, source in enumerate((query_weight, key_weight, value_weight))
    ]
    parts = []
    for part in range(own.shape[0] // WINDOW):
        place = pl.multiple_of(spots[0] + part * WINDOW, WINDOW)
        source = own.at[part * WINDOW : (part + 1) * WINDOW, :]
        parts.append(fetch(source, tokens.at[pl.ds(place, WINDOW), :]))
    for index, source in enumerate((other_0, other_1, other_2, other_3)):
        size = source.shape[0]
        place = pl.multiple_of(spots[1 + index], 128)
        parts.append(fetch(source, tokens.at[pl.ds(place, size), :]))
    given_copy = fetch(out_grad_in, out_grad)
    late = [
        fetch(tracker_in, tracker),
        fetch(tracker_copy_in, tracker_copy),
        fetch(tracker_mixed_in, tracker_mixed),
        fetch(grad_prev_in, grad_prev),
    ]
    for copy in ready:
        copy.wait()
    half = own.shape[0]
    for place, group in ((spots[0], parts[:-4]), (half - spots[0], parts[-4:])):
        for copy in group:
            copy.wait()
        window = pl.ds(pl.multiple_of(place, half), half)
        result = jnp.dot(tokens[window, :], joined[...], preferred_element_type=jnp.float32)
        projected[window, :] = result.astype(jnp.bfloat16)
    given_copy.wait()
    total[...] = jnp.zeros_like(total)

    lane = lax.broadcasted_iota(jnp.int32, (1, width), 1)
    first_head = (lane < HD).astype(jnp.float32).astype(jnp.bfloat16)
    second_head = (lane >= HD).astype(jnp.float32).astype(jnp.bfloat16)
    scale = HD ** (-0.5)

    @pl.loop(0, IMAGES, unroll=6)
    def _(image):
        start = starts[image]
        end = starts[image + 1]
        base = pl.multiple_of(jnp.minimum((start // 16) * 16, rows - WINDOW), 16)
        window = pl.ds(base, WINDOW)
        query = projected[window, :width] * scale
        keyed = projected[window, width : 2 * width]
        valued = projected[window, 2 * width :]
        given = out_grad[window, :]
        queries = jnp.concatenate([query * first_head, query * second_head], axis=0)
        givens = jnp.concatenate([given * first_head, given * second_head], axis=0)
        over_columns = (((1,), (1,)), ((), ()))
        over_rows = (((0,), (0,)), ((), ()))
        scores = lax.dot_general(keyed, queries, over_columns, preferred_element_type=jnp.float32)
        out_proj = lax.dot_general(valued, givens, over_columns, preferred_element_type=jnp.float32)
        row = lax.broadcasted_iota(jnp.int32, scores.shape, 0) + base
        scores = jnp.where((row >= start) & (row < end), scores, -1e30)
        exponent = jnp.exp(scores - jnp.max(scores, axis=0, keepdims=True))
        inverse = 1.0 / jnp.sum(exponent, axis=0, keepdims=True)
        centre = jnp.sum(exponent * out_proj, axis=0, keepdims=True) * inverse
        score_grad = ((exponent * (inverse * scale)) * (out_proj - centre)).astype(jnp.bfloat16)
        both = lax.dot_general(keyed, score_grad, over_rows, preferred_element_type=jnp.float32)
        query_grad = jnp.concatenate([both[:HD, :WINDOW], both[HD:, WINDOW:]], axis=0)
        column = lax.broadcasted_iota(jnp.int32, query_grad.shape, 1) + base
        query_grad = jnp.where((column >= start) & (column < end), query_grad, 0.0)
        total[...] += jnp.dot(
            query_grad.astype(jnp.bfloat16), tokens[window, :], preferred_element_type=jnp.float32
        )

    gradient = (total[...].T * rows ** (-0.5)).astype(jnp.bfloat16)
    grad_new[...] = gradient
    for copy in late:
        copy.wait()
    copy_value = tracker_copy[...].astype(jnp.float32)
    fresh = (
        tracker[...].astype(jnp.float32)
        + mixing_rate * (tracker_mixed[...].astype(jnp.float32) - copy_value)
        + gradient.astype(jnp.float32)
        - grad_prev[...].astype(jnp.float32)
    ).astype(jnp.bfloat16)
    tracker_new[...] = fresh
    change[...] = fresh.astype(jnp.float32) - copy_value
    update[...] = jnp.zeros_like(update)
    for index in range(picks.shape[0]):
        place = picks[index]
        row = change[pl.ds(place, 1), :]
        kept[pl.ds(index, 1), :] = row
        update[pl.ds(place, 1), :] = row
    tracker_copy_new[...] = (copy_value + update[...]).astype(jnp.bfloat16)


def gradient_step(spots, starts, picks, *arrays):
    rows, width = arrays[8].shape
    depth = arrays[0].shape[1]
    scalars = [pl.BlockSpec(memory_space=pltpu.SMEM)] * 3
    whole = pl.BlockSpec(memory_space=pltpu.VMEM)
    narrow = jax.ShapeDtypeStruct((rows, width), jnp.bfloat16)
    return pl.pallas_call(
        gradient_kernel,
        out_shape=(
            narrow,
            narrow,
            narrow,
            jax.ShapeDtypeStruct((rows, width), jnp.float32),
            jax.ShapeDtypeStruct((picks.shape[0], width), jnp.float32),
        ),
        in_specs=scalars + [pl.BlockSpec(memory_space=pl.ANY)] * len(arrays),
        out_specs=(whole,) * 5,
        scratch_shapes=[
            pltpu.VMEM((depth, 3 * width), jnp.bfloat16),
            pltpu.VMEM((rows, depth), jnp.bfloat16),
            pltpu.VMEM((rows, 3 * width), jnp.bfloat16),
            pltpu.VMEM((width, depth), jnp.float32),
            pltpu.VMEM((rows, width), jnp.float32),
        ]
        + [pltpu.VMEM((rows, width), jnp.bfloat16)] * 5
        + [pltpu.SemaphoreType.DMA((14,))],
        compiler_params=pltpu.CompilerParams(vmem_limit_bytes=52 * 2**20),
        cost_estimate=pl.CostEstimate(
            flops=2 * 10**9, bytes_accessed=8 * 10**6, transcendentals=8 * 10**5
        ),
    )(spots, starts, picks, *arrays)


def mix_kernel(far_picks, near_picks, far, near, update, mixed, mixed_new, total):
    total[...] = update[...]
    for picks, values in ((near_picks, near), (far_picks, far)):
        for low in range(0, picks.shape[0], 8):
            places = [pl.ds(picks[low + step], 1) for step in range(8)]
            sums = [
                total[place, :] + values[low + step : low + step + 1, :]
                for step, place in enumerate(places)
            ]
            for place, row in zip(places, sums):
                total[place, :] = row
    mixed_new[...] = (mixed[...].astype(jnp.float32) + total[...] / 3.0).astype(jnp.bfloat16)


def mix_step(far_picks, near_picks, *arrays):
    scalars = [pl.BlockSpec(memory_space=pltpu.SMEM)] * 2
    whole = pl.BlockSpec(memory_space=pltpu.VMEM)
    rows, width = arrays[3].shape
    return pl.pallas_call(
        mix_kernel,
        out_shape=jax.ShapeDtypeStruct((rows, width), jnp.bfloat16),
        in_specs=scalars + [whole] * len(arrays),
        out_specs=whole,
        scratch_shapes=[pltpu.VMEM((rows, width), jnp.float32)],
        compiler_params=pltpu.CompilerParams(vmem_limit_bytes=8 * 2**20),
        cost_estimate=pl.CostEstimate(flops=10**6, bytes_accessed=10**6, transcendentals=0),
    )(far_picks, near_picks, *arrays)


def per_device(
    weights,
    copies,
    copies_mixed,
    tracker,
    tracker_copy,
    tracker_mixed,
    grad_prev,
    tokens,
    image_ids,
    key_weight,
    value_weight,
    out_grad,
    row_picks,
):
    model_width = weights.shape[1]
    high = lax.axis_index("tp_0")
    place = lax.axis_index("tp_1")
    height = tokens.shape[1]
    half = height * lax.axis_size("tp_1")
    other = lax.ppermute(tokens[0], "tp_0", [(0, 1), (1, 0)])
    own_half = spread_tokens(tokens[0])
    picks = neighbour_picks(row_picks)
    own_picks = picks[0]
    copy_value = copies[0].astype(jnp.float32)
    mixed_value = copies_mixed[0].astype(jnp.float32)
    weights_new = (
        weights[0]
        + mixing_rate * (mixed_value - copy_value)
        - step_rate * tracker[0].astype(jnp.float32)
    )
    param_values = select_rows(own_picks[0], weights_new - copy_value)
    copies_new = (copy_value + place_rows(own_picks[0], param_values, model_width)).astype(
        jnp.bfloat16
    )
    param_sent = param_values.astype(jnp.bfloat16)
    param_near, param_far = swaps(param_sent)
    param_received = jnp.concatenate((param_sent, param_far, param_near), axis=0).astype(
        jnp.float32
    )
    mixed_new = (mixed_value + mix_stream(param_received, [own_picks[0], picks[2][0], picks[1][0]], model_width)).astype(
        jnp.bfloat16
    )
    partial_sums = gap_rows(mixed_new, copies_new)
    own_half, other = lax.optimization_barrier((own_half, other))
    blocks = pass_tokens(other)
    _, partial_sums = lax.optimization_barrier((other, partial_sums))
    partial_sums = spread_rows(partial_sums, ("blk_1", "tp_0"))
    spots = [high * half] + [
        (1 - high) * half + ((place - shift) % len(blocks)) * height for shift in range(len(blocks))
    ]
    query_weight = (weights_new * model_width ** (-0.5)).astype(jnp.bfloat16)
    grad_new, tracker_new, tracker_copy_new, update, tracker_values = gradient_step(
        jnp.stack(spots).astype(jnp.int32),
        image_starts(image_ids[0]),
        own_picks[1],
        own_half,
        *blocks,
        query_weight,
        key_weight,
        value_weight,
        out_grad[0],
        tracker[0],
        tracker_copy[0],
        tracker_mixed[0],
        grad_prev[0],
    )
    tracker_values, partial_sums = lax.optimization_barrier((tracker_values, partial_sums))
    near, far = swaps(tracker_values)
    partial_sums = spread_rows(
        jnp.sum(partial_sums, axis=0, keepdims=True), ("blk_0", "blk_2", "tp_1")
    )
    tracker_mixed_new = mix_step(
        picks[2][1], picks[1][1], far, near, update, tracker_mixed[0]
    )
    tracker_mixed_new, partial_sums = lax.optimization_barrier((tracker_mixed_new, partial_sums))
    consensus = consensus_of(partial_sums, model_width)
    return (
        weights_new[None],
        copies_new[None],
        mixed_new[None],
        tracker_new[None],
        tracker_copy_new[None],
        tracker_mixed_new[None],
        grad_new[None],
        consensus,
    )


def solution(mesh):
    finer = Mesh(mesh.devices.reshape(4, 8, 2, 2, 4), ("blk_0", "blk_1", "blk_2", "tp_0", "tp_1"))
    in_specs = (
        P(BLK, None, TP),
        P(BLK, None, TP),
        P(BLK, None, TP),
        P(BLK, None, TP),
        P(BLK, None, TP),
        P(BLK, None, TP),
        P(BLK, None, TP),
        P(BLK, TP, None),
        P(BLK, None),
        P(None, TP),
        P(None, TP),
        P(BLK, None, TP),
        P(),
    )
    out_specs = (
        P(BLK, None, TP),
        P(BLK, None, TP),
        P(BLK, None, TP),
        P(BLK, None, TP),
        P(BLK, None, TP),
        P(BLK, None, TP),
        P(BLK, None, TP),
        P(),
    )
    return jax.shard_map(
        per_device, mesh=finer, in_specs=in_specs, out_specs=out_specs, check_vma=False
    )
```

```python
import jax
import jax.numpy as jnp
from jax import lax
from jax.experimental import pallas as pl
from jax.experimental.pallas import tpu as pltpu
from jax.sharding import Mesh
from jax.sharding import PartitionSpec as P

HD = 64
IMAGES = 6
WINDOW = 256
BLK = ("blk_0", "blk_1", "blk_2")
TP = ("tp_0", "tp_1")


mixing_rate = 0.2
step_rate = 0.5


def swaps(value):
    count = lax.axis_size(BLK)
    near = [(r, r ^ 1) for r in range(count)]
    far = [(r, (r + 1) % count if r % 2 else (r - 1) % count) for r in range(count)]
    from_far = lax.ppermute(value, BLK, far)
    return lax.ppermute(value, BLK, near), from_far


def spread_rows(value, axes):
    count = lax.axis_size(axes)
    rows = jnp.broadcast_to(value, (count, value.shape[1]))
    return lax.all_to_all(rows, axes, 0, 0, tiled=True)


def spread_sum(value, axes):
    return jnp.sum(spread_rows(value, axes), axis=0, keepdims=True)


def spread_tokens(value):
    count = lax.axis_size("tp_1")
    blocks = jnp.broadcast_to(value, (count,) + value.shape)
    return lax.all_to_all(blocks, "tp_1", 0, 0, tiled=True).reshape(-1, value.shape[1])


def pass_tokens(value):
    count = lax.axis_size("tp_1")
    blocks = [value]
    for shift in range(1, count):
        pairs = [(i, (i + shift) % count) for i in range(count)]
        blocks.append(lax.ppermute(value, "tp_1", pairs))
    return blocks


def pick_matrix(picks, total_rows):
    columns = lax.broadcasted_iota(jnp.int32, (picks.shape[0], total_rows), 1)
    return (picks[:, None] == columns).astype(jnp.float32)


def select_rows(picks, field):
    return jnp.dot(pick_matrix(picks, field.shape[0]), field, precision=lax.Precision.HIGHEST)


def neighbour_picks(row_picks):
    count = lax.axis_size(BLK)
    rank = lax.axis_index(BLK)
    near = rank + 1 - 2 * (rank % 2)
    far = (rank - 1 + 2 * (rank % 2) + count) % count
    return [
        lax.dynamic_index_in_dim(row_picks, place, 0, keepdims=False) for place in (rank, near, far)
    ]


def consensus_of(partial_sums, width):
    return jnp.sum(partial_sums) / float(lax.axis_size(BLK) * width * width)


def image_starts(ids):
    marks = lax.broadcasted_iota(jnp.int32, (8, ids.shape[0]), 0)
    return jnp.sum((ids[None, :] < marks).astype(jnp.int32), axis=1)


def gradient_kernel(
    spots,
    starts,
    picks,
    own,
    other_0,
    other_1,
    other_2,
    other_3,
    query_weight,
    key_weight,
    value_weight,
    out_grad_in,
    tracker_in,
    tracker_copy_in,
    tracker_mixed_in,
    grad_prev_in,
    grad_new,
    tracker_new,
    tracker_copy_new,
    update,
    kept,
    joined,
    tokens,
    projected,
    total,
    change,
    out_grad,
    tracker,
    tracker_copy,
    tracker_mixed,
    grad_prev,
    sems,
):
    width = query_weight.shape[1]
    rows = tokens.shape[0]
    copies = []

    def fetch(source, target):
        copy = pltpu.make_async_copy(source, target, sems.at[len(copies)])
        copy.start()
        copies.append(copy)
        return copy

    ready = [
        fetch(source, joined.at[:, index * width : (index + 1) * width])
        for index, source in enumerate((query_weight, key_weight, value_weight))
    ]
    parts = []
    for part in range(own.shape[0] // WINDOW):
        place = pl.multiple_of(spots[0] + part * WINDOW, WINDOW)
        source = own.at[part * WINDOW : (part + 1) * WINDOW, :]
        parts.append(fetch(source, tokens.at[pl.ds(place, WINDOW), :]))
    for index, source in enumerate((other_0, other_1, other_2, other_3)):
        size = source.shape[0]
        place = pl.multiple_of(spots[1 + index], 128)
        parts.append(fetch(source, tokens.at[pl.ds(place, size), :]))
    given_copy = fetch(out_grad_in, out_grad)
    late = [
        fetch(tracker_in, tracker),
        fetch(tracker_copy_in, tracker_copy),
        fetch(tracker_mixed_in, tracker_mixed),
        fetch(grad_prev_in, grad_prev),
    ]
    for copy in ready:
        copy.wait()
    half = own.shape[0]
    for place, group in ((spots[0], parts[:-4]), (half - spots[0], parts[-4:])):
        for copy in group:
            copy.wait()
        window = pl.ds(pl.multiple_of(place, half), half)
        result = jnp.dot(tokens[window, :], joined[...], preferred_element_type=jnp.float32)
        projected[window, :] = result.astype(jnp.bfloat16)
    given_copy.wait()
    total[...] = jnp.zeros_like(total)

    lane = lax.broadcasted_iota(jnp.int32, (1, width), 1)
    first_head = (lane < HD).astype(jnp.float32).astype(jnp.bfloat16)
    second_head = (lane >= HD).astype(jnp.float32).astype(jnp.bfloat16)
    scale = HD ** (-0.5)

    @pl.loop(0, IMAGES, unroll=6)
    def _(image):
        start = starts[image]
        end = starts[image + 1]
        base = pl.multiple_of(jnp.minimum((start // 16) * 16, rows - WINDOW), 16)
        window = pl.ds(base, WINDOW)
        query = projected[window, :width] * scale
        keyed = projected[window, width : 2 * width]
        valued = projected[window, 2 * width :]
        given = out_grad[window, :]
        queries = jnp.concatenate([query * first_head, query * second_head], axis=0)
        givens = jnp.concatenate([given * first_head, given * second_head], axis=0)
        over_columns = (((1,), (1,)), ((), ()))
        over_rows = (((0,), (0,)), ((), ()))
        scores = lax.dot_general(keyed, queries, over_columns, preferred_element_type=jnp.float32)
        out_proj = lax.dot_general(valued, givens, over_columns, preferred_element_type=jnp.float32)
        row = lax.broadcasted_iota(jnp.int32, scores.shape, 0) + base
        scores = jnp.where((row >= start) & (row < end), scores, -1e30)
        exponent = jnp.exp(scores - jnp.max(scores, axis=0, keepdims=True))
        inverse = 1.0 / jnp.sum(exponent, axis=0, keepdims=True)
        centre = jnp.sum(exponent * out_proj, axis=0, keepdims=True) * inverse
        score_grad = ((exponent * (inverse * scale)) * (out_proj - centre)).astype(jnp.bfloat16)
        both = lax.dot_general(keyed, score_grad, over_rows, preferred_element_type=jnp.float32)
        query_grad = jnp.concatenate([both[:HD, :WINDOW], both[HD:, WINDOW:]], axis=0)
        column = lax.broadcasted_iota(jnp.int32, query_grad.shape, 1) + base
        query_grad = jnp.where((column >= start) & (column < end), query_grad, 0.0)
        total[...] += jnp.dot(
            query_grad.astype(jnp.bfloat16), tokens[window, :], preferred_element_type=jnp.float32
        )

    gradient = (total[...].T * rows ** (-0.5)).astype(jnp.bfloat16)
    grad_new[...] = gradient
    for copy in late:
        copy.wait()
    copy_value = tracker_copy[...].astype(jnp.float32)
    fresh = (
        tracker[...].astype(jnp.float32)
        + mixing_rate * (tracker_mixed[...].astype(jnp.float32) - copy_value)
        + gradient.astype(jnp.float32)
        - grad_prev[...].astype(jnp.float32)
    ).astype(jnp.bfloat16)
    tracker_new[...] = fresh
    change[...] = fresh.astype(jnp.float32) - copy_value
    update[...] = jnp.zeros_like(update)
    for index in range(picks.shape[0]):
        place = picks[index]
        row = change[pl.ds(place, 1), :]
        kept[pl.ds(index, 1), :] = row
        update[pl.ds(place, 1), :] = row
    tracker_copy_new[...] = (copy_value + update[...]).astype(jnp.bfloat16)


def gradient_step(spots, starts, picks, *arrays):
    rows, width = arrays[8].shape
    depth = arrays[0].shape[1]
    scalars = [pl.BlockSpec(memory_space=pltpu.SMEM)] * 3
    whole = pl.BlockSpec(memory_space=pltpu.VMEM)
    narrow = jax.ShapeDtypeStruct((rows, width), jnp.bfloat16)
    return pl.pallas_call(
        gradient_kernel,
        out_shape=(
            narrow,
            narrow,
            narrow,
            jax.ShapeDtypeStruct((rows, width), jnp.float32),
            jax.ShapeDtypeStruct((picks.shape[0], width), jnp.float32),
        ),
        in_specs=scalars + [pl.BlockSpec(memory_space=pl.ANY)] * len(arrays),
        out_specs=(whole,) * 5,
        scratch_shapes=[
            pltpu.VMEM((depth, 3 * width), jnp.bfloat16),
            pltpu.VMEM((rows, depth), jnp.bfloat16),
            pltpu.VMEM((rows, 3 * width), jnp.bfloat16),
            pltpu.VMEM((width, depth), jnp.float32),
            pltpu.VMEM((rows, width), jnp.float32),
        ]
        + [pltpu.VMEM((rows, width), jnp.bfloat16)] * 5
        + [pltpu.SemaphoreType.DMA((14,))],
        compiler_params=pltpu.CompilerParams(vmem_limit_bytes=52 * 2**20),
        cost_estimate=pl.CostEstimate(
            flops=2 * 10**9, bytes_accessed=8 * 10**6, transcendentals=8 * 10**5
        ),
    )(spots, starts, picks, *arrays)


def scatter_rows(total, picks, values):
    for low in range(0, picks.shape[0], 8):
        places = [pl.ds(picks[low + step], 1) for step in range(8)]
        sums = [
            total[place, :] + values[low + step : low + step + 1, :]
            for step, place in enumerate(places)
        ]
        for place, row in zip(places, sums):
            total[place, :] = row


def param_kernel(
    own_picks,
    far_picks,
    near_picks,
    own,
    far,
    near,
    copies,
    mixed,
    copies_new,
    mixed_new,
    gaps,
    total,
):
    total[...] = jnp.zeros_like(total)
    scatter_rows(total, own_picks, own[...])
    fresh = (copies[...].astype(jnp.float32) + total[...]).astype(jnp.bfloat16)
    copies_new[...] = fresh
    scatter_rows(total, far_picks, far[...].astype(jnp.float32))
    scatter_rows(total, near_picks, near[...].astype(jnp.float32))
    blend = (mixed[...].astype(jnp.float32) + total[...] / 3.0).astype(jnp.bfloat16)
    mixed_new[...] = blend
    gap = blend.astype(jnp.float32) - fresh.astype(jnp.float32)
    gaps[...] = jnp.sum(gap * gap, axis=0, keepdims=True)


def param_step(own_picks, far_picks, near_picks, *arrays):
    scalars = [pl.BlockSpec(memory_space=pltpu.SMEM)] * 3
    whole = pl.BlockSpec(memory_space=pltpu.VMEM)
    rows, width = arrays[3].shape
    narrow = jax.ShapeDtypeStruct((rows, width), jnp.bfloat16)
    return pl.pallas_call(
        param_kernel,
        out_shape=(narrow, narrow, jax.ShapeDtypeStruct((1, width), jnp.float32)),
        in_specs=scalars + [whole] * len(arrays),
        out_specs=(whole,) * 3,
        scratch_shapes=[pltpu.VMEM((rows, width), jnp.float32)],
        compiler_params=pltpu.CompilerParams(vmem_limit_bytes=8 * 2**20),
        cost_estimate=pl.CostEstimate(flops=1000, bytes_accessed=1000, transcendentals=0),
    )(own_picks, far_picks, near_picks, *arrays)


def mix_kernel(far_picks, near_picks, far, near, update, mixed, mixed_new, total):
    total[...] = update[...]
    scatter_rows(total, far_picks, far[...])
    scatter_rows(total, near_picks, near[...])
    mixed_new[...] = (mixed[...].astype(jnp.float32) + total[...] / 3.0).astype(jnp.bfloat16)


def mix_step(far_picks, near_picks, *arrays):
    scalars = [pl.BlockSpec(memory_space=pltpu.SMEM)] * 2
    whole = pl.BlockSpec(memory_space=pltpu.VMEM)
    rows, width = arrays[3].shape
    return pl.pallas_call(
        mix_kernel,
        out_shape=jax.ShapeDtypeStruct((rows, width), jnp.bfloat16),
        in_specs=scalars + [whole] * len(arrays),
        out_specs=whole,
        scratch_shapes=[pltpu.VMEM((rows, width), jnp.float32)],
        compiler_params=pltpu.CompilerParams(vmem_limit_bytes=8 * 2**20),
        cost_estimate=pl.CostEstimate(flops=10**6, bytes_accessed=10**6, transcendentals=0),
    )(far_picks, near_picks, *arrays)


def per_device(
    weights,
    copies,
    copies_mixed,
    tracker,
    tracker_copy,
    tracker_mixed,
    grad_prev,
    tokens,
    image_ids,
    key_weight,
    value_weight,
    out_grad,
    row_picks,
):
    model_width = weights.shape[1]
    high = lax.axis_index("tp_0")
    place = lax.axis_index("tp_1")
    height = tokens.shape[1]
    half = height * lax.axis_size("tp_1")
    other = lax.ppermute(tokens[0], "tp_0", [(0, 1), (1, 0)])
    own_half = spread_tokens(tokens[0])
    picks = neighbour_picks(row_picks)
    own_picks = picks[0]
    copy_value = copies[0].astype(jnp.float32)
    mixed_value = copies_mixed[0].astype(jnp.float32)
    weights_new = (
        weights[0]
        + mixing_rate * (mixed_value - copy_value)
        - step_rate * tracker[0].astype(jnp.float32)
    )
    param_values = select_rows(own_picks[0], weights_new - copy_value)
    param_near, param_far = swaps(param_values.astype(jnp.bfloat16))
    param_picks = (picks[0][0], picks[2][0], picks[1][0])
    query_weight = (weights_new * model_width ** (-0.5)).astype(jnp.bfloat16)
    early = (query_weight, image_starts(image_ids[0]), [kept[1] for kept in picks], param_picks)
    own_half, other, early = lax.optimization_barrier((own_half, other, early))
    query_weight, starts, later_picks, param_picks = early
    copies_new, mixed_new, partial_sums = param_step(
        *param_picks,
        param_values,
        param_far,
        param_near,
        copies[0],
        copies_mixed[0],
    )
    blocks = pass_tokens(other)
    _, partial_sums = lax.optimization_barrier((other, partial_sums))
    partial_sums = spread_rows(partial_sums, ("blk_1", "tp_0"))
    spots = [high * half] + [
        (1 - high) * half + ((place - shift) % len(blocks)) * height for shift in range(len(blocks))
    ]
    grad_new, tracker_new, tracker_copy_new, update, tracker_values = gradient_step(
        jnp.stack(spots).astype(jnp.int32),
        starts,
        later_picks[0],
        own_half,
        *blocks,
        query_weight,
        key_weight,
        value_weight,
        out_grad[0],
        tracker[0],
        tracker_copy[0],
        tracker_mixed[0],
        grad_prev[0],
    )
    near, far = swaps(tracker_values)
    _, partial_sums = lax.optimization_barrier((tracker_values, partial_sums))
    partial_sums = spread_rows(
        jnp.sum(partial_sums, axis=0, keepdims=True), ("blk_0", "blk_2", "tp_1")
    )
    tracker_mixed_new = mix_step(
        later_picks[2], later_picks[1], far, near, update, tracker_mixed[0]
    )
    tracker_mixed_new, partial_sums = lax.optimization_barrier((tracker_mixed_new, partial_sums))
    consensus = consensus_of(partial_sums, model_width)
    return (
        weights_new[None],
        copies_new[None],
        mixed_new[None],
        tracker_new[None],
        tracker_copy_new[None],
        tracker_mixed_new[None],
        grad_new[None],
        consensus,
    )


def solution(mesh):
    finer = Mesh(mesh.devices.reshape(4, 8, 2, 2, 4), ("blk_0", "blk_1", "blk_2", "tp_0", "tp_1"))
    in_specs = (
        P(BLK, None, TP),
        P(BLK, None, TP),
        P(BLK, None, TP),
        P(BLK, None, TP),
        P(BLK, None, TP),
        P(BLK, None, TP),
        P(BLK, None, TP),
        P(BLK, TP, None),
        P(BLK, None),
        P(None, TP),
        P(None, TP),
        P(BLK, None, TP),
        P(),
    )
    out_specs = (
        P(BLK, None, TP),
        P(BLK, None, TP),
        P(BLK, None, TP),
        P(BLK, None, TP),
        P(BLK, None, TP),
        P(BLK, None, TP),
        P(BLK, None, TP),
        P(),
    )
    return jax.shard_map(
        per_device, mesh=finer, in_specs=in_specs, out_specs=out_specs, check_vma=False
    )
```

```python
import jax
import jax.numpy as jnp
from jax import lax
from jax.experimental import pallas as pl
from jax.experimental.pallas import tpu as pltpu
from jax.sharding import Mesh
from jax.sharding import PartitionSpec as P

HD = 64
IMAGES = 6
WINDOW = 256
BLK = ("blk_0", "blk_1", "blk_2")
TP = ("tp_0", "tp_1")


mixing_rate = 0.2
step_rate = 0.5


def swaps(value):
    count = lax.axis_size(BLK)
    near = [(r, r ^ 1) for r in range(count)]
    far = [(r, (r + 1) % count if r % 2 else (r - 1) % count) for r in range(count)]
    from_far = lax.ppermute(value, BLK, far)
    return lax.ppermute(value, BLK, near), from_far


def spread_rows(value, axes):
    count = lax.axis_size(axes)
    rows = jnp.broadcast_to(value, (count, value.shape[1]))
    return lax.all_to_all(rows, axes, 0, 0, tiled=True)


def spread_sum(value, axes):
    return jnp.sum(spread_rows(value, axes), axis=0, keepdims=True)


def spread_tokens(value):
    count = lax.axis_size("tp_1")
    blocks = jnp.broadcast_to(value, (count,) + value.shape)
    return lax.all_to_all(blocks, "tp_1", 0, 0, tiled=True).reshape(-1, value.shape[1])


def pass_tokens(value):
    count = lax.axis_size("tp_1")
    blocks = [value]
    for shift in range(1, count):
        pairs = [(i, (i + shift) % count) for i in range(count)]
        blocks.append(lax.ppermute(value, "tp_1", pairs))
    return blocks


def pick_matrix(picks, total_rows):
    columns = lax.broadcasted_iota(jnp.int32, (picks.shape[0], total_rows), 1)
    return (picks[:, None] == columns).astype(jnp.float32)


def select_rows(picks, field):
    return jnp.dot(pick_matrix(picks, field.shape[0]), field, precision=lax.Precision.HIGHEST)


def neighbour_picks(row_picks):
    count = lax.axis_size(BLK)
    rank = lax.axis_index(BLK)
    near = rank + 1 - 2 * (rank % 2)
    far = (rank - 1 + 2 * (rank % 2) + count) % count
    return [
        lax.dynamic_index_in_dim(row_picks, place, 0, keepdims=False) for place in (rank, near, far)
    ]


def consensus_of(partial_sums, width):
    return jnp.sum(partial_sums) / float(lax.axis_size(BLK) * width * width)


def image_starts(ids):
    marks = lax.broadcasted_iota(jnp.int32, (8, ids.shape[0]), 0)
    return jnp.sum((ids[None, :] < marks).astype(jnp.int32), axis=1)


def fresh_tracker(tracker, copy_value, mixed, gradient, grad_prev):
    return (
        tracker.astype(jnp.float32)
        + mixing_rate * (mixed.astype(jnp.float32) - copy_value)
        + gradient.astype(jnp.float32)
        - grad_prev.astype(jnp.float32)
    ).astype(jnp.bfloat16)


def tracker_kernel(
    picks,
    kept,
    gradient,
    tracker,
    tracker_copy,
    tracker_mixed,
    grad_prev,
    tracker_new,
    tracker_copy_new,
    update,
):
    copy_value = tracker_copy[...].astype(jnp.float32)
    tracker_new[...] = fresh_tracker(
        tracker[...], copy_value, tracker_mixed[...], gradient[...], grad_prev[...]
    )
    update[...] = jnp.zeros_like(update)
    scatter_rows(update, picks, kept[...])
    tracker_copy_new[...] = (copy_value + update[...]).astype(jnp.bfloat16)


def tracker_step(picks, *arrays):
    whole = pl.BlockSpec(memory_space=pltpu.VMEM)
    rows, width = arrays[1].shape
    narrow = jax.ShapeDtypeStruct((rows, width), jnp.bfloat16)
    return pl.pallas_call(
        tracker_kernel,
        out_shape=(narrow, narrow, jax.ShapeDtypeStruct((rows, width), jnp.float32)),
        in_specs=[pl.BlockSpec(memory_space=pltpu.SMEM)] + [whole] * len(arrays),
        out_specs=(whole,) * 3,
        compiler_params=pltpu.CompilerParams(vmem_limit_bytes=8 * 2**20),
        cost_estimate=pl.CostEstimate(
            flops=10**6, bytes_accessed=3 * 10**6, transcendentals=0
        ),
    )(picks, *arrays)


def gradient_kernel(
    spots,
    starts,
    picks,
    own,
    other_0,
    other_1,
    other_2,
    other_3,
    query_weight,
    key_weight,
    value_weight,
    out_grad_in,
    tracker_in,
    tracker_copy_in,
    tracker_mixed_in,
    grad_prev_in,
    grad_new,
    kept,
    joined,
    tokens,
    projected,
    total,
    change,
    out_grad,
    tracker,
    tracker_copy,
    tracker_mixed,
    grad_prev,
    sems,
):
    width = query_weight.shape[1]
    rows = tokens.shape[0]
    copies = []

    def fetch(source, target):
        copy = pltpu.make_async_copy(source, target, sems.at[len(copies)])
        copy.start()
        copies.append(copy)
        return copy

    ready = [
        fetch(source, joined.at[:, index * width : (index + 1) * width])
        for index, source in enumerate((query_weight, key_weight, value_weight))
    ]
    parts = []
    for part in range(own.shape[0] // WINDOW):
        place = pl.multiple_of(spots[0] + part * WINDOW, WINDOW)
        source = own.at[part * WINDOW : (part + 1) * WINDOW, :]
        parts.append(fetch(source, tokens.at[pl.ds(place, WINDOW), :]))
    for index, source in enumerate((other_0, other_1, other_2, other_3)):
        size = source.shape[0]
        place = pl.multiple_of(spots[1 + index], 128)
        parts.append(fetch(source, tokens.at[pl.ds(place, size), :]))
    given_copy = fetch(out_grad_in, out_grad)
    late = [
        fetch(tracker_in, tracker),
        fetch(tracker_copy_in, tracker_copy),
        fetch(tracker_mixed_in, tracker_mixed),
        fetch(grad_prev_in, grad_prev),
    ]
    for copy in ready:
        copy.wait()
    half = own.shape[0]
    for place, group in ((spots[0], parts[:-4]), (half - spots[0], parts[-4:])):
        for copy in group:
            copy.wait()
        window = pl.ds(pl.multiple_of(place, half), half)
        result = jnp.dot(tokens[window, :], joined[...], preferred_element_type=jnp.float32)
        projected[window, :] = result.astype(jnp.bfloat16)
    given_copy.wait()
    total[...] = jnp.zeros_like(total)

    lane = lax.broadcasted_iota(jnp.int32, (1, width), 1)
    first_head = (lane < HD).astype(jnp.float32).astype(jnp.bfloat16)
    second_head = (lane >= HD).astype(jnp.float32).astype(jnp.bfloat16)
    scale = HD ** (-0.5)

    @pl.loop(0, IMAGES, unroll=6)
    def _(image):
        start = starts[image]
        end = starts[image + 1]
        base = pl.multiple_of(jnp.minimum((start // 16) * 16, rows - WINDOW), 16)
        window = pl.ds(base, WINDOW)
        query = projected[window, :width] * scale
        keyed = projected[window, width : 2 * width]
        valued = projected[window, 2 * width :]
        given = out_grad[window, :]
        queries = jnp.concatenate([query * first_head, query * second_head], axis=0)
        givens = jnp.concatenate([given * first_head, given * second_head], axis=0)
        over_columns = (((1,), (1,)), ((), ()))
        over_rows = (((0,), (0,)), ((), ()))
        scores = lax.dot_general(keyed, queries, over_columns, preferred_element_type=jnp.float32)
        out_proj = lax.dot_general(valued, givens, over_columns, preferred_element_type=jnp.float32)
        row = lax.broadcasted_iota(jnp.int32, scores.shape, 0) + base
        scores = jnp.where((row >= start) & (row < end), scores, -1e30)
        exponent = jnp.exp(scores - jnp.max(scores, axis=0, keepdims=True))
        inverse = 1.0 / jnp.sum(exponent, axis=0, keepdims=True)
        centre = jnp.sum(exponent * out_proj, axis=0, keepdims=True) * inverse
        score_grad = ((exponent * (inverse * scale)) * (out_proj - centre)).astype(jnp.bfloat16)
        both = lax.dot_general(keyed, score_grad, over_rows, preferred_element_type=jnp.float32)
        query_grad = jnp.concatenate([both[:HD, :WINDOW], both[HD:, WINDOW:]], axis=0)
        column = lax.broadcasted_iota(jnp.int32, query_grad.shape, 1) + base
        query_grad = jnp.where((column >= start) & (column < end), query_grad, 0.0)
        total[...] += jnp.dot(
            query_grad.astype(jnp.bfloat16), tokens[window, :], preferred_element_type=jnp.float32
        )

    gradient = (total[...].T * rows ** (-0.5)).astype(jnp.bfloat16)
    grad_new[...] = gradient
    for copy in late:
        copy.wait()
    copy_value = tracker_copy[...].astype(jnp.float32)
    fresh = fresh_tracker(tracker[...], copy_value, tracker_mixed[...], gradient, grad_prev[...])
    change[...] = fresh.astype(jnp.float32) - copy_value
    for index in range(picks.shape[0]):
        kept[pl.ds(index, 1), :] = change[pl.ds(picks[index], 1), :]


def gradient_step(spots, starts, picks, *arrays):
    rows, width = arrays[8].shape
    depth = arrays[0].shape[1]
    scalars = [pl.BlockSpec(memory_space=pltpu.SMEM)] * 3
    whole = pl.BlockSpec(memory_space=pltpu.VMEM)
    narrow = jax.ShapeDtypeStruct((rows, width), jnp.bfloat16)
    return pl.pallas_call(
        gradient_kernel,
        out_shape=(narrow, jax.ShapeDtypeStruct((picks.shape[0], width), jnp.float32)),
        in_specs=scalars + [pl.BlockSpec(memory_space=pl.ANY)] * len(arrays),
        out_specs=(whole,) * 2,
        scratch_shapes=[
            pltpu.VMEM((depth, 3 * width), jnp.bfloat16),
            pltpu.VMEM((rows, depth), jnp.bfloat16),
            pltpu.VMEM((rows, 3 * width), jnp.bfloat16),
            pltpu.VMEM((width, depth), jnp.float32),
            pltpu.VMEM((rows, width), jnp.float32),
        ]
        + [pltpu.VMEM((rows, width), jnp.bfloat16)] * 5
        + [pltpu.SemaphoreType.DMA((14,))],
        compiler_params=pltpu.CompilerParams(vmem_limit_bytes=52 * 2**20),
        cost_estimate=pl.CostEstimate(
            flops=2 * 10**9, bytes_accessed=8 * 10**6, transcendentals=8 * 10**5
        ),
    )(spots, starts, picks, *arrays)


def scatter_rows(total, picks, values):
    for low in range(0, picks.shape[0], 8):
        places = [pl.ds(picks[low + step], 1) for step in range(8)]
        sums = [
            total[place, :] + values[low + step : low + step + 1, :]
            for step, place in enumerate(places)
        ]
        for place, row in zip(places, sums):
            total[place, :] = row


def param_kernel(
    own_picks,
    far_picks,
    near_picks,
    own,
    far,
    near,
    copies,
    mixed,
    copies_new,
    mixed_new,
    gaps,
    total,
):
    total[...] = jnp.zeros_like(total)
    scatter_rows(total, own_picks, own[...])
    fresh = (copies[...].astype(jnp.float32) + total[...]).astype(jnp.bfloat16)
    copies_new[...] = fresh
    scatter_rows(total, far_picks, far[...].astype(jnp.float32))
    scatter_rows(total, near_picks, near[...].astype(jnp.float32))
    blend = (mixed[...].astype(jnp.float32) + total[...] / 3.0).astype(jnp.bfloat16)
    mixed_new[...] = blend
    gap = blend.astype(jnp.float32) - fresh.astype(jnp.float32)
    gaps[...] = jnp.sum(gap * gap, axis=0, keepdims=True)


def param_step(own_picks, far_picks, near_picks, *arrays):
    scalars = [pl.BlockSpec(memory_space=pltpu.SMEM)] * 3
    whole = pl.BlockSpec(memory_space=pltpu.VMEM)
    rows, width = arrays[3].shape
    narrow = jax.ShapeDtypeStruct((rows, width), jnp.bfloat16)
    return pl.pallas_call(
        param_kernel,
        out_shape=(narrow, narrow, jax.ShapeDtypeStruct((1, width), jnp.float32)),
        in_specs=scalars + [whole] * len(arrays),
        out_specs=(whole,) * 3,
        scratch_shapes=[pltpu.VMEM((rows, width), jnp.float32)],
        compiler_params=pltpu.CompilerParams(vmem_limit_bytes=8 * 2**20),
        cost_estimate=pl.CostEstimate(flops=1000, bytes_accessed=1000, transcendentals=0),
    )(own_picks, far_picks, near_picks, *arrays)


def mix_kernel(far_picks, near_picks, far, near, update, mixed, mixed_new, total):
    total[...] = update[...]
    scatter_rows(total, far_picks, far[...])
    scatter_rows(total, near_picks, near[...])
    mixed_new[...] = (mixed[...].astype(jnp.float32) + total[...] / 3.0).astype(jnp.bfloat16)


def mix_step(far_picks, near_picks, *arrays):
    scalars = [pl.BlockSpec(memory_space=pltpu.SMEM)] * 2
    whole = pl.BlockSpec(memory_space=pltpu.VMEM)
    rows, width = arrays[3].shape
    return pl.pallas_call(
        mix_kernel,
        out_shape=jax.ShapeDtypeStruct((rows, width), jnp.bfloat16),
        in_specs=scalars + [whole] * len(arrays),
        out_specs=whole,
        scratch_shapes=[pltpu.VMEM((rows, width), jnp.float32)],
        compiler_params=pltpu.CompilerParams(vmem_limit_bytes=8 * 2**20),
        cost_estimate=pl.CostEstimate(flops=10**6, bytes_accessed=10**6, transcendentals=0),
    )(far_picks, near_picks, *arrays)


def per_device(
    weights,
    copies,
    copies_mixed,
    tracker,
    tracker_copy,
    tracker_mixed,
    grad_prev,
    tokens,
    image_ids,
    key_weight,
    value_weight,
    out_grad,
    row_picks,
):
    model_width = weights.shape[1]
    high = lax.axis_index("tp_0")
    place = lax.axis_index("tp_1")
    height = tokens.shape[1]
    half = height * lax.axis_size("tp_1")
    other = lax.ppermute(tokens[0], "tp_0", [(0, 1), (1, 0)])
    own_half = spread_tokens(tokens[0])
    picks = neighbour_picks(row_picks)
    own_picks = picks[0]
    copy_value = copies[0].astype(jnp.float32)
    mixed_value = copies_mixed[0].astype(jnp.float32)
    weights_new = (
        weights[0]
        + mixing_rate * (mixed_value - copy_value)
        - step_rate * tracker[0].astype(jnp.float32)
    )
    param_values = select_rows(own_picks[0], weights_new - copy_value)
    param_near, param_far = swaps(param_values.astype(jnp.bfloat16))
    param_picks = (picks[0][0], picks[2][0], picks[1][0])
    own_half, other, starts, later_picks = lax.optimization_barrier(
        (own_half, other, image_starts(image_ids[0]), [kept[1] for kept in picks])
    )
    copies_new, mixed_new, partial_sums = param_step(
        *param_picks,
        param_values,
        param_far,
        param_near,
        copies[0],
        copies_mixed[0],
    )
    blocks = pass_tokens(other)
    _, partial_sums = lax.optimization_barrier((other, partial_sums))
    partial_sums = spread_rows(partial_sums, ("blk_1", "tp_0"))
    spots = [high * half] + [
        (1 - high) * half + ((place - shift) % len(blocks)) * height for shift in range(len(blocks))
    ]
    query_weight = (weights_new * model_width ** (-0.5)).astype(jnp.bfloat16)
    grad_new, tracker_values = gradient_step(
        jnp.stack(spots).astype(jnp.int32),
        starts,
        later_picks[0],
        own_half,
        *blocks,
        query_weight,
        key_weight,
        value_weight,
        out_grad[0],
        tracker[0],
        tracker_copy[0],
        tracker_mixed[0],
        grad_prev[0],
    )
    near, far = swaps(tracker_values)
    tracker_new, tracker_copy_new, update = tracker_step(
        later_picks[0],
        tracker_values,
        grad_new,
        tracker[0],
        tracker_copy[0],
        tracker_mixed[0],
        grad_prev[0],
    )
    _, partial_sums = lax.optimization_barrier((tracker_values, partial_sums))
    partial_sums = spread_rows(
        jnp.sum(partial_sums, axis=0, keepdims=True), ("blk_0", "blk_2", "tp_1")
    )
    tracker_mixed_new = mix_step(
        later_picks[2], later_picks[1], far, near, update, tracker_mixed[0]
    )
    tracker_mixed_new, partial_sums = lax.optimization_barrier((tracker_mixed_new, partial_sums))
    consensus = consensus_of(partial_sums, model_width)
    return (
        weights_new[None],
        copies_new[None],
        mixed_new[None],
        tracker_new[None],
        tracker_copy_new[None],
        tracker_mixed_new[None],
        grad_new[None],
        consensus,
    )


def solution(mesh):
    finer = Mesh(mesh.devices.reshape(4, 8, 2, 2, 4), ("blk_0", "blk_1", "blk_2", "tp_0", "tp_1"))
    in_specs = (
        P(BLK, None, TP),
        P(BLK, None, TP),
        P(BLK, None, TP),
        P(BLK, None, TP),
        P(BLK, None, TP),
        P(BLK, None, TP),
        P(BLK, None, TP),
        P(BLK, TP, None),
        P(BLK, None),
        P(None, TP),
        P(None, TP),
        P(BLK, None, TP),
        P(),
    )
    out_specs = (
        P(BLK, None, TP),
        P(BLK, None, TP),
        P(BLK, None, TP),
        P(BLK, None, TP),
        P(BLK, None, TP),
        P(BLK, None, TP),
        P(BLK, None, TP),
        P(),
    )
    return jax.shard_map(
        per_device, mesh=finer, in_specs=in_specs, out_specs=out_specs, check_vma=False
    )
```

```python
import jax
import jax.numpy as jnp
from jax import lax
from jax.experimental import pallas as pl
from jax.experimental.pallas import tpu as pltpu
from jax.sharding import Mesh
from jax.sharding import PartitionSpec as P

HD = 64
IMAGES = 6
WINDOW = 256
BLK = ("blk_0", "blk_1", "blk_2")
TP = ("tp_0", "tp_1")


mixing_rate = 0.2
step_rate = 0.5


def near_swap(value):
    count = lax.axis_size(BLK)
    return lax.ppermute(value, BLK, [(r, r ^ 1) for r in range(count)])


def far_swap(value):
    count = lax.axis_size(BLK)
    pairs = [(r, (r + 1) % count if r % 2 else (r - 1) % count) for r in range(count)]
    return lax.ppermute(value, BLK, pairs)


def spread_rows(value, axes):
    count = lax.axis_size(axes)
    rows = jnp.broadcast_to(value, (count, value.shape[1]))
    return lax.all_to_all(rows, axes, 0, 0, tiled=True)


def spread_sum(value, axes):
    return jnp.sum(spread_rows(value, axes), axis=0, keepdims=True)


def spread_tokens(value):
    count = lax.axis_size("tp_1")
    blocks = jnp.broadcast_to(value, (count,) + value.shape)
    return lax.all_to_all(blocks, "tp_1", 0, 0, tiled=True).reshape(-1, value.shape[1])


def pass_tokens(value):
    count = lax.axis_size("tp_1")
    blocks = [value]
    for shift in range(1, count):
        pairs = [(i, (i + shift) % count) for i in range(count)]
        blocks.append(lax.ppermute(value, "tp_1", pairs))
    return blocks


def pick_matrix(picks, total_rows):
    columns = lax.broadcasted_iota(jnp.int32, (picks.shape[0], total_rows), 1)
    return (picks[:, None] == columns).astype(jnp.float32)


def select_rows(picks, field):
    return jnp.dot(pick_matrix(picks, field.shape[0]), field, precision=lax.Precision.HIGHEST)


def neighbour_picks(row_picks):
    count = lax.axis_size(BLK)
    rank = lax.axis_index(BLK)
    near = rank + 1 - 2 * (rank % 2)
    far = (rank - 1 + 2 * (rank % 2) + count) % count
    return [
        lax.dynamic_index_in_dim(row_picks, place, 0, keepdims=False) for place in (rank, near, far)
    ]


def consensus_of(partial_sums, width):
    return jnp.sum(partial_sums) / float(lax.axis_size(BLK) * width * width)


def image_starts(ids):
    marks = lax.broadcasted_iota(jnp.int32, (8, ids.shape[0]), 0)
    return jnp.sum((ids[None, :] < marks).astype(jnp.int32), axis=1)


def fresh_tracker(tracker, copy_value, mixed, gradient, grad_prev):
    return (
        tracker.astype(jnp.float32)
        + mixing_rate * (mixed.astype(jnp.float32) - copy_value)
        + gradient.astype(jnp.float32)
        - grad_prev.astype(jnp.float32)
    ).astype(jnp.bfloat16)


def tracker_kernel(
    picks,
    kept,
    gradient,
    tracker,
    tracker_copy,
    tracker_mixed,
    grad_prev,
    tracker_new,
    tracker_copy_new,
    update,
):
    copy_value = tracker_copy[...].astype(jnp.float32)
    tracker_new[...] = fresh_tracker(
        tracker[...], copy_value, tracker_mixed[...], gradient[...], grad_prev[...]
    )
    update[...] = jnp.zeros_like(update)
    scatter_rows(update, picks, kept[...])
    tracker_copy_new[...] = (copy_value + update[...]).astype(jnp.bfloat16)


def tracker_step(picks, *arrays):
    whole = pl.BlockSpec(memory_space=pltpu.VMEM)
    rows, width = arrays[1].shape
    narrow = jax.ShapeDtypeStruct((rows, width), jnp.bfloat16)
    return pl.pallas_call(
        tracker_kernel,
        out_shape=(narrow, narrow, jax.ShapeDtypeStruct((rows, width), jnp.float32)),
        in_specs=[pl.BlockSpec(memory_space=pltpu.SMEM)] + [whole] * len(arrays),
        out_specs=(whole,) * 3,
        compiler_params=pltpu.CompilerParams(vmem_limit_bytes=8 * 2**20),
        cost_estimate=pl.CostEstimate(
            flops=10**6, bytes_accessed=3 * 10**6, transcendentals=0
        ),
    )(picks, *arrays)


def gradient_kernel(
    spots,
    starts,
    picks,
    own,
    other_0,
    other_1,
    other_2,
    other_3,
    query_weight,
    key_weight,
    value_weight,
    out_grad_in,
    tracker_in,
    tracker_copy_in,
    tracker_mixed_in,
    grad_prev_in,
    grad_new,
    kept,
    joined,
    tokens,
    projected,
    total,
    change,
    out_grad,
    tracker,
    tracker_copy,
    tracker_mixed,
    grad_prev,
    sems,
):
    width = query_weight.shape[1]
    rows = tokens.shape[0]
    copies = []

    def fetch(source, target):
        copy = pltpu.make_async_copy(source, target, sems.at[len(copies)])
        copy.start()
        copies.append(copy)
        return copy

    ready = [
        fetch(source, joined.at[:, index * width : (index + 1) * width])
        for index, source in enumerate((query_weight, key_weight, value_weight))
    ]
    half = own.shape[0]
    other_parts = []
    for index, source in enumerate((other_0, other_1, other_2, other_3)):
        size = source.shape[0]
        place = pl.multiple_of(spots[1 + index], 128)
        other_parts.append(fetch(source, tokens.at[pl.ds(place, size), :]))
    place = pl.multiple_of(spots[0], half)
    own_parts = [fetch(own, tokens.at[pl.ds(place, half), :])]
    given_copy = fetch(out_grad_in, out_grad)
    late = [
        fetch(tracker_in, tracker),
        fetch(tracker_copy_in, tracker_copy),
        fetch(tracker_mixed_in, tracker_mixed),
        fetch(grad_prev_in, grad_prev),
    ]
    for copy in ready:
        copy.wait()
    for place, group in ((half - spots[0], other_parts), (spots[0], own_parts)):
        for copy in group:
            copy.wait()
        window = pl.ds(pl.multiple_of(place, half), half)
        result = jnp.dot(tokens[window, :], joined[...], preferred_element_type=jnp.float32)
        projected[window, :] = result.astype(jnp.bfloat16)
    given_copy.wait()
    total[...] = jnp.zeros_like(total)

    lane = lax.broadcasted_iota(jnp.int32, (1, width), 1)
    first_head = (lane < HD).astype(jnp.float32).astype(jnp.bfloat16)
    second_head = (lane >= HD).astype(jnp.float32).astype(jnp.bfloat16)
    scale = HD ** (-0.5)

    @pl.loop(0, IMAGES, unroll=6)
    def _(image):
        start = starts[image]
        end = starts[image + 1]
        base = pl.multiple_of(jnp.minimum((start // 16) * 16, rows - WINDOW), 16)
        window = pl.ds(base, WINDOW)
        query = projected[window, :width] * scale
        keyed = projected[window, width : 2 * width]
        valued = projected[window, 2 * width :]
        given = out_grad[window, :]
        queries = jnp.concatenate([query * first_head, query * second_head], axis=0)
        givens = jnp.concatenate([given * first_head, given * second_head], axis=0)
        over_columns = (((1,), (1,)), ((), ()))
        over_rows = (((0,), (0,)), ((), ()))
        scores = lax.dot_general(keyed, queries, over_columns, preferred_element_type=jnp.float32)
        out_proj = lax.dot_general(valued, givens, over_columns, preferred_element_type=jnp.float32)
        row = lax.broadcasted_iota(jnp.int32, scores.shape, 0) + base
        scores = jnp.where((row >= start) & (row < end), scores, -1e30)
        exponent = jnp.exp(scores - jnp.max(scores, axis=0, keepdims=True))
        inverse = 1.0 / jnp.sum(exponent, axis=0, keepdims=True)
        centre = jnp.sum(exponent * out_proj, axis=0, keepdims=True) * inverse
        score_grad = ((exponent * (inverse * scale)) * (out_proj - centre)).astype(jnp.bfloat16)
        both = lax.dot_general(keyed, score_grad, over_rows, preferred_element_type=jnp.float32)
        query_grad = jnp.concatenate([both[:HD, :WINDOW], both[HD:, WINDOW:]], axis=0)
        column = lax.broadcasted_iota(jnp.int32, query_grad.shape, 1) + base
        query_grad = jnp.where((column >= start) & (column < end), query_grad, 0.0)
        total[...] += jnp.dot(
            query_grad.astype(jnp.bfloat16), tokens[window, :], preferred_element_type=jnp.float32
        )

    gradient = (total[...].T * rows ** (-0.5)).astype(jnp.bfloat16)
    grad_new[...] = gradient
    for copy in late:
        copy.wait()
    copy_value = tracker_copy[...].astype(jnp.float32)
    fresh = fresh_tracker(tracker[...], copy_value, tracker_mixed[...], gradient, grad_prev[...])
    change[...] = fresh.astype(jnp.float32) - copy_value
    for index in range(picks.shape[0]):
        kept[pl.ds(index, 1), :] = change[pl.ds(picks[index], 1), :]


def gradient_step(spots, starts, picks, *arrays):
    rows, width = arrays[8].shape
    depth = arrays[0].shape[1]
    scalars = [pl.BlockSpec(memory_space=pltpu.SMEM)] * 3
    whole = pl.BlockSpec(memory_space=pltpu.VMEM)
    narrow = jax.ShapeDtypeStruct((rows, width), jnp.bfloat16)
    return pl.pallas_call(
        gradient_kernel,
        out_shape=(narrow, jax.ShapeDtypeStruct((picks.shape[0], width), jnp.float32)),
        in_specs=scalars + [pl.BlockSpec(memory_space=pl.ANY)] * len(arrays),
        out_specs=(whole,) * 2,
        scratch_shapes=[
            pltpu.VMEM((depth, 3 * width), jnp.bfloat16),
            pltpu.VMEM((rows, depth), jnp.bfloat16),
            pltpu.VMEM((rows, 3 * width), jnp.bfloat16),
            pltpu.VMEM((width, depth), jnp.float32),
            pltpu.VMEM((rows, width), jnp.float32),
        ]
        + [pltpu.VMEM((rows, width), jnp.bfloat16)] * 5
        + [pltpu.SemaphoreType.DMA((14,))],
        compiler_params=pltpu.CompilerParams(vmem_limit_bytes=52 * 2**20),
        cost_estimate=pl.CostEstimate(
            flops=2 * 10**9, bytes_accessed=8 * 10**6, transcendentals=8 * 10**5
        ),
    )(spots, starts, picks, *arrays)


def scatter_rows(total, picks, values):
    for low in range(0, picks.shape[0], 8):
        places = [pl.ds(picks[low + step], 1) for step in range(8)]
        sums = [
            total[place, :] + values[low + step : low + step + 1, :]
            for step, place in enumerate(places)
        ]
        for place, row in zip(places, sums):
            total[place, :] = row


def param_kernel(
    own_picks,
    far_picks,
    near_picks,
    own,
    far,
    near,
    copies,
    mixed,
    copies_new,
    mixed_new,
    gaps,
    total,
):
    total[...] = jnp.zeros_like(total)
    scatter_rows(total, own_picks, own[...])
    fresh = (copies[...].astype(jnp.float32) + total[...]).astype(jnp.bfloat16)
    copies_new[...] = fresh
    scatter_rows(total, far_picks, far[...].astype(jnp.float32))
    scatter_rows(total, near_picks, near[...].astype(jnp.float32))
    blend = (mixed[...].astype(jnp.float32) + total[...] / 3.0).astype(jnp.bfloat16)
    mixed_new[...] = blend
    gap = blend.astype(jnp.float32) - fresh.astype(jnp.float32)
    gaps[...] = jnp.broadcast_to(jnp.sum(gap * gap, axis=0, keepdims=True), gaps.shape)


def param_step(count, own_picks, far_picks, near_picks, *arrays):
    scalars = [pl.BlockSpec(memory_space=pltpu.SMEM)] * 3
    whole = pl.BlockSpec(memory_space=pltpu.VMEM)
    rows, width = arrays[3].shape
    narrow = jax.ShapeDtypeStruct((rows, width), jnp.bfloat16)
    return pl.pallas_call(
        param_kernel,
        out_shape=(narrow, narrow, jax.ShapeDtypeStruct((count, width), jnp.float32)),
        in_specs=scalars + [whole] * len(arrays),
        out_specs=(whole,) * 3,
        scratch_shapes=[pltpu.VMEM((rows, width), jnp.float32)],
        compiler_params=pltpu.CompilerParams(vmem_limit_bytes=8 * 2**20),
        cost_estimate=pl.CostEstimate(flops=1000, bytes_accessed=1000, transcendentals=0),
    )(own_picks, far_picks, near_picks, *arrays)


def mix_kernel(far_picks, near_picks, far, near, update, mixed, mixed_new, total):
    total[...] = update[...]
    scatter_rows(total, far_picks, far[...])
    scatter_rows(total, near_picks, near[...])
    mixed_new[...] = (mixed[...].astype(jnp.float32) + total[...] / 3.0).astype(jnp.bfloat16)


def mix_step(far_picks, near_picks, *arrays):
    scalars = [pl.BlockSpec(memory_space=pltpu.SMEM)] * 2
    whole = pl.BlockSpec(memory_space=pltpu.VMEM)
    rows, width = arrays[3].shape
    return pl.pallas_call(
        mix_kernel,
        out_shape=jax.ShapeDtypeStruct((rows, width), jnp.bfloat16),
        in_specs=scalars + [whole] * len(arrays),
        out_specs=whole,
        scratch_shapes=[pltpu.VMEM((rows, width), jnp.float32)],
        compiler_params=pltpu.CompilerParams(vmem_limit_bytes=8 * 2**20),
        cost_estimate=pl.CostEstimate(flops=10**6, bytes_accessed=10**6, transcendentals=0),
    )(far_picks, near_picks, *arrays)


def per_device(
    weights,
    copies,
    copies_mixed,
    tracker,
    tracker_copy,
    tracker_mixed,
    grad_prev,
    tokens,
    image_ids,
    key_weight,
    value_weight,
    out_grad,
    row_picks,
):
    model_width = weights.shape[1]
    high = lax.axis_index("tp_0")
    place = lax.axis_index("tp_1")
    height = tokens.shape[1]
    half = height * lax.axis_size("tp_1")
    other = lax.ppermute(tokens[0], "tp_0", [(0, 1), (1, 0)])
    own_half = spread_tokens(tokens[0])
    picks = neighbour_picks(row_picks)
    own_picks = picks[0]
    copy_value = copies[0].astype(jnp.float32)
    mixed_value = copies_mixed[0].astype(jnp.float32)
    weights_new = (
        weights[0]
        + mixing_rate * (mixed_value - copy_value)
        - step_rate * tracker[0].astype(jnp.float32)
    )
    param_values = select_rows(own_picks[0], weights_new - copy_value)
    param_sent = param_values.astype(jnp.bfloat16)
    param_far, param_near = far_swap(param_sent), near_swap(param_sent)
    param_picks = (picks[0][0], picks[2][0], picks[1][0])
    own_half, other, starts, later_picks = lax.optimization_barrier(
        (own_half, other, image_starts(image_ids[0]), [kept[1] for kept in picks])
    )
    copies_new, mixed_new, partial_sums = param_step(
        lax.axis_size(("blk_1", "tp_0")),
        *param_picks,
        param_values,
        param_far,
        param_near,
        copies[0],
        copies_mixed[0],
    )
    blocks = pass_tokens(other)
    _, partial_sums = lax.optimization_barrier((other, partial_sums))
    partial_sums = lax.all_to_all(partial_sums, ("blk_1", "tp_0"), 0, 0, tiled=True)
    spots = [high * half] + [
        (1 - high) * half + ((place - shift) % len(blocks)) * height for shift in range(len(blocks))
    ]
    query_weight = (weights_new * model_width ** (-0.5)).astype(jnp.bfloat16)
    grad_new, tracker_values = gradient_step(
        jnp.stack(spots).astype(jnp.int32),
        starts,
        later_picks[0],
        own_half,
        *blocks,
        query_weight,
        key_weight,
        value_weight,
        out_grad[0],
        tracker[0],
        tracker_copy[0],
        tracker_mixed[0],
        grad_prev[0],
    )
    tracker_new, tracker_copy_new, update = tracker_step(
        later_picks[0],
        tracker_values,
        grad_new,
        tracker[0],
        tracker_copy[0],
        tracker_mixed[0],
        grad_prev[0],
    )
    far = far_swap(tracker_values)
    _, partial_sums = lax.optimization_barrier((tracker_values, partial_sums))
    partial_sums = jnp.sum(partial_sums, axis=0, keepdims=True)
    tracker_values, partial_sums = lax.optimization_barrier((tracker_values, partial_sums))
    near = near_swap(tracker_values)
    partial_sums = spread_rows(partial_sums, ("blk_0", "blk_2", "tp_1"))
    tracker_mixed_new = mix_step(
        later_picks[2], later_picks[1], far, near, update, tracker_mixed[0]
    )
    tracker_mixed_new, partial_sums = lax.optimization_barrier((tracker_mixed_new, partial_sums))
    consensus = consensus_of(partial_sums, model_width)
    return (
        weights_new[None],
        copies_new[None],
        mixed_new[None],
        tracker_new[None],
        tracker_copy_new[None],
        tracker_mixed_new[None],
        grad_new[None],
        consensus,
    )


def solution(mesh):
    finer = Mesh(mesh.devices.reshape(4, 8, 2, 2, 4), ("blk_0", "blk_1", "blk_2", "tp_0", "tp_1"))
    in_specs = (
        P(BLK, None, TP),
        P(BLK, None, TP),
        P(BLK, None, TP),
        P(BLK, None, TP),
        P(BLK, None, TP),
        P(BLK, None, TP),
        P(BLK, None, TP),
        P(BLK, TP, None),
        P(BLK, None),
        P(None, TP),
        P(None, TP),
        P(BLK, None, TP),
        P(),
    )
    out_specs = (
        P(BLK, None, TP),
        P(BLK, None, TP),
        P(BLK, None, TP),
        P(BLK, None, TP),
        P(BLK, None, TP),
        P(BLK, None, TP),
        P(BLK, None, TP),
        P(),
    )
    return jax.shard_map(
        per_device, mesh=finer, in_specs=in_specs, out_specs=out_specs, check_vma=False
    )
```

```python
import jax
import jax.numpy as jnp
from jax import lax
from jax.experimental import pallas as pl
from jax.experimental.pallas import tpu as pltpu
from jax.sharding import Mesh
from jax.sharding import PartitionSpec as P

HD = 64
IMAGES = 6
WINDOW = 256
BLK = ("blk_0", "blk_1", "blk_2")
TP = ("tp_0", "tp_1")


mixing_rate = 0.2
step_rate = 0.5


def near_swap(value):
    count = lax.axis_size(BLK)
    return lax.ppermute(value, BLK, [(r, r ^ 1) for r in range(count)])


def far_swap(value):
    count = lax.axis_size(BLK)
    pairs = [(r, (r + 1) % count if r % 2 else (r - 1) % count) for r in range(count)]
    return lax.ppermute(value, BLK, pairs)


def spread_rows(value, axes):
    count = lax.axis_size(axes)
    rows = jnp.broadcast_to(value, (count, value.shape[1]))
    return lax.all_to_all(rows, axes, 0, 0, tiled=True)


def spread_sum(value, axes):
    return jnp.sum(spread_rows(value, axes), axis=0, keepdims=True)


def spread_tokens(value):
    count = lax.axis_size("tp_1")
    blocks = jnp.broadcast_to(value, (count,) + value.shape)
    return lax.all_to_all(blocks, "tp_1", 0, 0, tiled=True).reshape(-1, value.shape[1])


def pass_tokens(value):
    count = lax.axis_size("tp_1")
    blocks = [value]
    for shift in range(1, count):
        pairs = [(i, (i + shift) % count) for i in range(count)]
        blocks.append(lax.ppermute(value, "tp_1", pairs))
    return blocks


def pick_matrix(picks, total_rows):
    columns = lax.broadcasted_iota(jnp.int32, (picks.shape[0], total_rows), 1)
    return (picks[:, None] == columns).astype(jnp.float32)


def select_rows(picks, field):
    return jnp.dot(pick_matrix(picks, field.shape[0]), field, precision=lax.Precision.HIGHEST)


def neighbour_picks(row_picks):
    count = lax.axis_size(BLK)
    rank = lax.axis_index(BLK)
    near = rank + 1 - 2 * (rank % 2)
    far = (rank - 1 + 2 * (rank % 2) + count) % count
    return [
        lax.dynamic_index_in_dim(row_picks, place, 0, keepdims=False) for place in (rank, near, far)
    ]


def consensus_of(partial_sums, width):
    return jnp.sum(partial_sums) / float(lax.axis_size(BLK) * width * width)


def image_starts(ids):
    marks = lax.broadcasted_iota(jnp.int32, (8, ids.shape[0]), 0)
    return jnp.sum((ids[None, :] < marks).astype(jnp.int32), axis=1)


def fresh_tracker(tracker, copy_value, mixed, gradient, grad_prev):
    return (
        tracker.astype(jnp.float32)
        + mixing_rate * (mixed.astype(jnp.float32) - copy_value)
        + gradient.astype(jnp.float32)
        - grad_prev.astype(jnp.float32)
    ).astype(jnp.bfloat16)


def tracker_kernel(
    picks,
    kept,
    gradient,
    tracker,
    tracker_copy,
    tracker_mixed,
    grad_prev,
    tracker_new,
    tracker_copy_new,
    update,
):
    copy_value = tracker_copy[...].astype(jnp.float32)
    tracker_new[...] = fresh_tracker(
        tracker[...], copy_value, tracker_mixed[...], gradient[...], grad_prev[...]
    )
    update[...] = jnp.zeros_like(update)
    scatter_rows(update, picks, kept[...])
    tracker_copy_new[...] = (copy_value + update[...]).astype(jnp.bfloat16)


def tracker_step(picks, *arrays):
    whole = pl.BlockSpec(memory_space=pltpu.VMEM)
    rows, width = arrays[1].shape
    narrow = jax.ShapeDtypeStruct((rows, width), jnp.bfloat16)
    return pl.pallas_call(
        tracker_kernel,
        out_shape=(narrow, narrow, jax.ShapeDtypeStruct((rows, width), jnp.float32)),
        in_specs=[pl.BlockSpec(memory_space=pltpu.SMEM)] + [whole] * len(arrays),
        out_specs=(whole,) * 3,
        compiler_params=pltpu.CompilerParams(vmem_limit_bytes=8 * 2**20),
        cost_estimate=pl.CostEstimate(
            flops=10**6, bytes_accessed=3 * 10**6, transcendentals=0
        ),
    )(picks, *arrays)


def gradient_kernel(
    spots,
    starts,
    picks,
    own,
    other_0,
    other_1,
    other_2,
    other_3,
    query_weight,
    key_weight,
    value_weight,
    out_grad_in,
    tracker_in,
    tracker_copy_in,
    tracker_mixed_in,
    grad_prev_in,
    grad_new,
    kept,
    joined,
    tokens,
    projected,
    total,
    change,
    out_grad,
    tracker,
    tracker_copy,
    tracker_mixed,
    grad_prev,
    sems,
):
    width = query_weight.shape[1]
    rows = tokens.shape[0]
    copies = []

    def fetch(source, target):
        copy = pltpu.make_async_copy(source, target, sems.at[len(copies)])
        copy.start()
        copies.append(copy)
        return copy

    ready = [
        fetch(source, joined.at[:, index * width : (index + 1) * width])
        for index, source in enumerate((query_weight, key_weight, value_weight))
    ]
    half = own.shape[0]
    other_parts = []
    for index, source in enumerate((other_0, other_1, other_2, other_3)):
        size = source.shape[0]
        place = pl.multiple_of(spots[1 + index], 128)
        other_parts.append(fetch(source, tokens.at[pl.ds(place, size), :]))
    place = pl.multiple_of(spots[0], half)
    own_parts = [fetch(own, tokens.at[pl.ds(place, half), :])]
    given_copy = fetch(out_grad_in, out_grad)
    late = [
        fetch(tracker_in, tracker),
        fetch(tracker_copy_in, tracker_copy),
        fetch(tracker_mixed_in, tracker_mixed),
        fetch(grad_prev_in, grad_prev),
    ]
    for copy in ready:
        copy.wait()
    for place, group in ((half - spots[0], other_parts), (spots[0], own_parts)):
        for copy in group:
            copy.wait()
        window = pl.ds(pl.multiple_of(place, half), half)
        result = jnp.dot(tokens[window, :], joined[...], preferred_element_type=jnp.float32)
        projected[window, :] = result.astype(jnp.bfloat16)
    given_copy.wait()
    total[...] = jnp.zeros_like(total)

    lane = lax.broadcasted_iota(jnp.int32, (1, width), 1)
    first_head = (lane < HD).astype(jnp.float32).astype(jnp.bfloat16)
    second_head = (lane >= HD).astype(jnp.float32).astype(jnp.bfloat16)
    scale = HD ** (-0.5)

    @pl.loop(0, IMAGES, unroll=6)
    def _(image):
        start = starts[image]
        end = starts[image + 1]
        base = pl.multiple_of(jnp.minimum((start // 16) * 16, rows - WINDOW), 16)
        window = pl.ds(base, WINDOW)
        query = projected[window, :width] * scale
        keyed = projected[window, width : 2 * width]
        valued = projected[window, 2 * width :]
        given = out_grad[window, :]
        queries = jnp.concatenate([query * first_head, query * second_head], axis=0)
        givens = jnp.concatenate([given * first_head, given * second_head], axis=0)
        over_columns = (((1,), (1,)), ((), ()))
        over_rows = (((0,), (0,)), ((), ()))
        scores = lax.dot_general(keyed, queries, over_columns, preferred_element_type=jnp.float32)
        out_proj = lax.dot_general(valued, givens, over_columns, preferred_element_type=jnp.float32)
        row = lax.broadcasted_iota(jnp.int32, scores.shape, 0) + base
        scores = jnp.where((row >= start) & (row < end), scores, -1e30)
        exponent = jnp.exp(scores - jnp.max(scores, axis=0, keepdims=True))
        inverse = 1.0 / jnp.sum(exponent, axis=0, keepdims=True)
        centre = jnp.sum(exponent * out_proj, axis=0, keepdims=True) * inverse
        score_grad = ((exponent * (inverse * scale)) * (out_proj - centre)).astype(jnp.bfloat16)
        both = lax.dot_general(keyed, score_grad, over_rows, preferred_element_type=jnp.float32)
        query_grad = jnp.concatenate([both[:HD, :WINDOW], both[HD:, WINDOW:]], axis=0)
        column = lax.broadcasted_iota(jnp.int32, query_grad.shape, 1) + base
        query_grad = jnp.where((column >= start) & (column < end), query_grad, 0.0)
        total[...] += jnp.dot(
            query_grad.astype(jnp.bfloat16), tokens[window, :], preferred_element_type=jnp.float32
        )

    gradient = (total[...].T * rows ** (-0.5)).astype(jnp.bfloat16)
    grad_new[...] = gradient
    for copy in late:
        copy.wait()
    copy_value = tracker_copy[...].astype(jnp.float32)
    fresh = fresh_tracker(tracker[...], copy_value, tracker_mixed[...], gradient, grad_prev[...])
    change[...] = fresh.astype(jnp.float32) - copy_value
    for index in range(picks.shape[0]):
        kept[pl.ds(index, 1), :] = change[pl.ds(picks[index], 1), :]


def gradient_step(spots, starts, picks, *arrays):
    rows, width = arrays[8].shape
    depth = arrays[0].shape[1]
    scalars = [pl.BlockSpec(memory_space=pltpu.SMEM)] * 3
    whole = pl.BlockSpec(memory_space=pltpu.VMEM)
    narrow = jax.ShapeDtypeStruct((rows, width), jnp.bfloat16)
    return pl.pallas_call(
        gradient_kernel,
        out_shape=(narrow, jax.ShapeDtypeStruct((picks.shape[0], width), jnp.float32)),
        in_specs=scalars + [pl.BlockSpec(memory_space=pl.ANY)] * len(arrays),
        out_specs=(whole,) * 2,
        scratch_shapes=[
            pltpu.VMEM((depth, 3 * width), jnp.bfloat16),
            pltpu.VMEM((rows, depth), jnp.bfloat16),
            pltpu.VMEM((rows, 3 * width), jnp.bfloat16),
            pltpu.VMEM((width, depth), jnp.float32),
            pltpu.VMEM((rows, width), jnp.float32),
        ]
        + [pltpu.VMEM((rows, width), jnp.bfloat16)] * 5
        + [pltpu.SemaphoreType.DMA((14,))],
        compiler_params=pltpu.CompilerParams(vmem_limit_bytes=52 * 2**20),
        cost_estimate=pl.CostEstimate(
            flops=2 * 10**9, bytes_accessed=8 * 10**6, transcendentals=8 * 10**5
        ),
    )(spots, starts, picks, *arrays)


def scatter_rows(total, picks, values):
    for low in range(0, picks.shape[0], 8):
        places = [pl.ds(picks[low + step], 1) for step in range(8)]
        sums = [
            total[place, :] + values[low + step : low + step + 1, :]
            for step, place in enumerate(places)
        ]
        for place, row in zip(places, sums):
            total[place, :] = row


def param_kernel(
    own_picks,
    far_picks,
    near_picks,
    own,
    far,
    near,
    copies,
    mixed,
    copies_new,
    mixed_new,
    gaps,
    total,
):
    total[...] = jnp.zeros_like(total)
    scatter_rows(total, own_picks, own[...])
    fresh = (copies[...].astype(jnp.float32) + total[...]).astype(jnp.bfloat16)
    copies_new[...] = fresh
    scatter_rows(total, far_picks, far[...].astype(jnp.float32))
    scatter_rows(total, near_picks, near[...].astype(jnp.float32))
    blend = (mixed[...].astype(jnp.float32) + total[...] / 3.0).astype(jnp.bfloat16)
    mixed_new[...] = blend
    gap = blend.astype(jnp.float32) - fresh.astype(jnp.float32)
    gaps[...] = jnp.broadcast_to(jnp.sum(gap * gap, axis=0, keepdims=True), gaps.shape)


def param_step(count, own_picks, far_picks, near_picks, *arrays):
    scalars = [pl.BlockSpec(memory_space=pltpu.SMEM)] * 3
    whole = pl.BlockSpec(memory_space=pltpu.VMEM)
    rows, width = arrays[3].shape
    narrow = jax.ShapeDtypeStruct((rows, width), jnp.bfloat16)
    return pl.pallas_call(
        param_kernel,
        out_shape=(narrow, narrow, jax.ShapeDtypeStruct((count, width), jnp.float32)),
        in_specs=scalars + [whole] * len(arrays),
        out_specs=(whole,) * 3,
        scratch_shapes=[pltpu.VMEM((rows, width), jnp.float32)],
        compiler_params=pltpu.CompilerParams(vmem_limit_bytes=8 * 2**20),
        cost_estimate=pl.CostEstimate(flops=1000, bytes_accessed=1000, transcendentals=0),
    )(own_picks, far_picks, near_picks, *arrays)


def mix_kernel(far_picks, near_picks, far, near, update, mixed, mixed_new, total):
    total[...] = update[...]
    scatter_rows(total, far_picks, far[...])
    scatter_rows(total, near_picks, near[...])
    mixed_new[...] = (mixed[...].astype(jnp.float32) + total[...] / 3.0).astype(jnp.bfloat16)


def mix_step(far_picks, near_picks, *arrays):
    scalars = [pl.BlockSpec(memory_space=pltpu.SMEM)] * 2
    whole = pl.BlockSpec(memory_space=pltpu.VMEM)
    rows, width = arrays[3].shape
    return pl.pallas_call(
        mix_kernel,
        out_shape=jax.ShapeDtypeStruct((rows, width), jnp.bfloat16),
        in_specs=scalars + [whole] * len(arrays),
        out_specs=whole,
        scratch_shapes=[pltpu.VMEM((rows, width), jnp.float32)],
        compiler_params=pltpu.CompilerParams(vmem_limit_bytes=8 * 2**20),
        cost_estimate=pl.CostEstimate(flops=10**6, bytes_accessed=10**6, transcendentals=0),
    )(far_picks, near_picks, *arrays)


def per_device(
    weights,
    copies,
    copies_mixed,
    tracker,
    tracker_copy,
    tracker_mixed,
    grad_prev,
    tokens,
    image_ids,
    key_weight,
    value_weight,
    out_grad,
    row_picks,
):
    model_width = weights.shape[1]
    high = lax.axis_index("tp_0")
    place = lax.axis_index("tp_1")
    height = tokens.shape[1]
    half = height * lax.axis_size("tp_1")
    other = lax.ppermute(tokens[0], "tp_0", [(0, 1), (1, 0)])
    own_half = spread_tokens(tokens[0])
    picks = neighbour_picks(row_picks)
    own_picks = picks[0]
    copy_value = copies[0].astype(jnp.float32)
    mixed_value = copies_mixed[0].astype(jnp.float32)
    weights_new = (
        weights[0]
        + mixing_rate * (mixed_value - copy_value)
        - step_rate * tracker[0].astype(jnp.float32)
    )
    param_values = select_rows(own_picks[0], weights_new - copy_value)
    param_sent = param_values.astype(jnp.bfloat16)
    param_far, param_near = far_swap(param_sent), near_swap(param_sent)
    param_picks = (picks[0][0], picks[2][0], picks[1][0])
    own_half, other, starts, later_picks = lax.optimization_barrier(
        (own_half, other, image_starts(image_ids[0]), [kept[1] for kept in picks])
    )
    copies_new, mixed_new, partial_sums = param_step(
        lax.axis_size(("blk_1", "tp_0")),
        *param_picks,
        param_values,
        param_far,
        param_near,
        copies[0],
        copies_mixed[0],
    )
    blocks = pass_tokens(other)
    _, partial_sums = lax.optimization_barrier((other, partial_sums))
    partial_sums = lax.all_to_all(partial_sums, ("blk_1", "tp_0"), 0, 0, tiled=True)
    spots = [high * half] + [
        (1 - high) * half + ((place - shift) % len(blocks)) * height for shift in range(len(blocks))
    ]
    query_weight = (weights_new * model_width ** (-0.5)).astype(jnp.bfloat16)
    grad_new, tracker_values = gradient_step(
        jnp.stack(spots).astype(jnp.int32),
        starts,
        later_picks[0],
        own_half,
        *blocks,
        query_weight,
        key_weight,
        value_weight,
        out_grad[0],
        tracker[0],
        tracker_copy[0],
        tracker_mixed[0],
        grad_prev[0],
    )
    tracker_new, tracker_copy_new, update = tracker_step(
        later_picks[0],
        tracker_values,
        grad_new,
        tracker[0],
        tracker_copy[0],
        tracker_mixed[0],
        grad_prev[0],
    )
    far = far_swap(tracker_values)
    _, partial_sums = lax.optimization_barrier((tracker_values, partial_sums))
    partial_sums = jnp.sum(partial_sums, axis=0, keepdims=True)
    tracker_values, update = lax.optimization_barrier((tracker_values, update))
    near = near_swap(tracker_values)
    partial_sums = spread_rows(partial_sums, ("blk_0", "blk_2", "tp_1"))
    tracker_mixed_new = mix_step(
        later_picks[2], later_picks[1], far, near, update, tracker_mixed[0]
    )
    tracker_mixed_new, partial_sums = lax.optimization_barrier((tracker_mixed_new, partial_sums))
    consensus = consensus_of(partial_sums, model_width)
    return (
        weights_new[None],
        copies_new[None],
        mixed_new[None],
        tracker_new[None],
        tracker_copy_new[None],
        tracker_mixed_new[None],
        grad_new[None],
        consensus,
    )


def solution(mesh):
    finer = Mesh(mesh.devices.reshape(4, 8, 2, 2, 4), ("blk_0", "blk_1", "blk_2", "tp_0", "tp_1"))
    in_specs = (
        P(BLK, None, TP),
        P(BLK, None, TP),
        P(BLK, None, TP),
        P(BLK, None, TP),
        P(BLK, None, TP),
        P(BLK, None, TP),
        P(BLK, None, TP),
        P(BLK, TP, None),
        P(BLK, None),
        P(None, TP),
        P(None, TP),
        P(BLK, None, TP),
        P(),
    )
    out_specs = (
        P(BLK, None, TP),
        P(BLK, None, TP),
        P(BLK, None, TP),
        P(BLK, None, TP),
        P(BLK, None, TP),
        P(BLK, None, TP),
        P(BLK, None, TP),
        P(),
    )
    return jax.shard_map(
        per_device, mesh=finer, in_specs=in_specs, out_specs=out_specs, check_vma=False
    )
```
